32 devices in a mesh: dp: 8 (over y, x, core), rep: 4 (over z).
Axes of the slice: x: 2, y: 2, z: 4, core: 2. Of those that a mesh axis runs over, the one named last changes fastest.
Arguments:
- clips: bfloat16 [32, 1024, 256], P(('dp', 'rep')), may hold values from -6 to 6
- cotangent: bfloat16 [32, 1024, 256], P(('dp', 'rep')), may hold values from -0.59765625 to 0.59765625
- alphas: float32 [2, 256], replicated, may hold values from 0.5 to 4
- weights: bfloat16 [524288], replicated, may hold values from -0.125 to 0.125
- master: float32 [524288], P('dp'), may hold values from -2 to 2
- first_moment: float32 [524288], P('dp'), may hold values from -6 to 6
- second_moment: float32 [524288], P('dp'), may hold values from 0.05 to 2
Outputs:
- new_weights: bfloat16 [524288], replicated
- new_master: float32 [524288], P('dp')
- new_first: float32 [524288], P('dp')
- new_second: float32 [524288], P('dp')
The draws below stay inside these ranges and needn't reach their ends.
All inputs are finite; a program needn't handle non-finite values.
Results may differ from the reference program's by a relative error of at most 0.0013.
Values may be sent and summed in bfloat16 or wider, within the bound.
A program may use at most 64 MiB of HBM per device.

```python
import math
import jax
import jax.numpy as jnp
from jax import lax

CH = 256
TAPS = 7
DILATION = 3
FRAMES = 1024
CLIPS = 32
PARAMS = 524288


def shard_levels(key, extent, shards, smallest, high):
    factor_of = 1.0
    for dim, shards_of in shards:
        steps = jax.random.uniform(jax.random.fold_in(jax.random.fold_in(key, 6), dim), (shards_of,), jnp.float32, smallest / len(shards), high / len(shards))
        factor_of = factor_of * jnp.repeat(jnp.exp(steps), extent[dim] // shards_of).reshape((-1,) + (1,) * (len(extent) - 1 - dim))
    return factor_of


def centred(rng, shape, scale, bound, shards=(), dtype=jnp.bfloat16):
    level = shard_levels(rng, shape, shards, -0.22, 0.18) if shards else 1.0
    entries = jax.random.normal(rng, shape, jnp.float32) * scale * level
    return jnp.minimum(jnp.maximum(entries, -bound), bound).astype(dtype)


def setup_inputs(seed: int = 0) -> dict:
    keys = jax.random.split(jax.random.key(seed), 8)
    clips = centred(keys[0], (CLIPS, FRAMES, CH), 1.0, 6.0, ((0, 32),))
    cotangent = centred(keys[1], (CLIPS, FRAMES, CH), 0.1, 0.59765625, ((0, 32),))
    alphas = jnp.clip(jnp.exp(jax.random.uniform(keys[2], (2, CH), jnp.float32, math.log(0.5), math.log(4.0))), 0.5, 4.0)
    weights = centred(keys[3], (PARAMS,), (TAPS * CH) ** -0.5, 0.125)
    master = centred(keys[4], (PARAMS,), 0.3, 2.0, ((0, 8),), jnp.float32)
    first_moment = centred(keys[5], (PARAMS,), 1.0, 6.0, ((0, 8),), jnp.float32)
    second_moment = jnp.clip(jnp.exp(math.log(2.0) - 3.6888794 * jax.random.uniform(keys[6], (PARAMS,), jnp.float32) ** shard_levels(keys[6], (PARAMS,), ((0, 8),), -0.2, 0.2)), 0.05, 2.0)
    return dict(clips=clips, cotangent=cotangent, alphas=alphas, weights=weights, master=master, first_moment=first_moment, second_moment=second_moment)


BIAS_ONE = 0.9999734386011124
BIAS_TWO = 0.09520785288629041

def snake(values, alpha):
    return values + jnp.sin(alpha * values) ** 2 / alpha

def clip_grads(clip, cot, alphas, weights):
    split = TAPS * CH * CH
    w_dilated = weights[:split].reshape(TAPS * CH, CH)
    w_point = weights[split:].reshape(CH, CH)
    first = snake(clip.astype(jnp.float32), alphas[0]).astype(jnp.bfloat16)
    reach = DILATION * (TAPS // 2)
    padded = jnp.pad(first, ((reach, reach), (0, 0)))
    windows = jnp.concatenate([padded[k * DILATION:k * DILATION + FRAMES] for k in range(TAPS)], axis=1)
    hidden = jnp.dot(windows, w_dilated, preferred_element_type=jnp.float32)
    second = snake(hidden, alphas[1]).astype(jnp.bfloat16)
    point_grad = jnp.dot(second.T, cot, preferred_element_type=jnp.float32)
    back = jnp.dot(cot, w_point.T, preferred_element_type=jnp.float32)
    d_hidden = (back * (1.0 + jnp.sin(2.0 * alphas[1] * hidden))).astype(jnp.bfloat16)
    dilated_grad = jnp.dot(windows.T, d_hidden, preferred_element_type=jnp.float32)
    return jnp.concatenate([dilated_grad.reshape(-1), point_grad.reshape(-1)])

def adam_update(gradient, master, first_moment, second_moment):
    new_first = 0.9 * first_moment + 0.1 * gradient
    new_second = 0.999 * second_moment + 0.001 * gradient * gradient
    new_master = master - 0.001 * (new_first / BIAS_ONE) / (jnp.sqrt(new_second / BIAS_TWO) + 1e-08)
    return (new_master, new_first, new_second)

def reference(clips, cotangent, alphas, weights, master, first_moment, second_moment):

    def accumulate(total, pair):
        return (total + clip_grads(pair[0], pair[1], alphas, weights), None)
    gradient, unused = lax.scan(accumulate, jnp.zeros((PARAMS,), jnp.float32), (clips, cotangent))
    new_master, new_first, new_second = adam_update(gradient, master, first_moment, second_moment)
    return (new_master.astype(jnp.bfloat16), new_master, new_first, new_second)
```

```python
import functools

import jax
import jax.numpy as jnp
from jax import lax
from jax.experimental import pallas as pl
from jax.experimental.pallas import tpu as pltpu
from jax.sharding import PartitionSpec as P

TAPS = 7
DILATION = 3
LANES = 128

BIAS_ONE = 0.9999734386011124
BIAS_TWO = 0.09520785288629041

PI_A = 3.140625
PI_B = 9.67502593994140625e-4
PI_C = 1.509957990978376432e-7
INV_PI = 0.3183098861837907

SIN = (-0.16666659712791443, 0.008333083242177963, -0.00019810810044873506, 2.6083068860316416e-06)
COS = (-0.5, 0.04166664183139801, -0.001388839678838849, 2.4761575332377106e-05, -2.607200428883516e-07)


def reduced(u):
    k = jnp.round(u * INV_PI)
    return ((u - k * PI_A) - k * PI_B) - k * PI_C


def sin_of(r, r2):
    return r + r * (r2 * (SIN[0] + r2 * (SIN[1] + r2 * (SIN[2] + r2 * SIN[3]))))


def cos_of(r2):
    return 1.0 + r2 * (COS[0] + r2 * (COS[1] + r2 * (COS[2] + r2 * (COS[3] + r2 * COS[4]))))


def dot(a, b, dims):
    return lax.dot_general(a, b, (dims, ((), ())), preferred_element_type=jnp.float32)


def adam(gradient, master, first_moment, second_moment):
    new_first = 0.9 * first_moment + 0.1 * gradient
    new_second = 0.999 * second_moment + 0.001 * gradient * gradient
    new_master = master - 0.001 * (new_first / BIAS_ONE) / (jnp.sqrt(new_second / BIAS_TWO) + 1e-08)
    return new_master, new_first, new_second


def step_kernel(
    plan,
    clip_hbm, cot_hbm, alpha_ref, w_hbm, ma_hbm, m1_hbm, m2_hbm,
    ow_hbm, oma_hbm, om1_hbm, om2_hbm,
    clip, cot, w_lin, w32, w_mat, ma, m1, m2,
    padded, win, lhs, grad, pair_buf, xy_buf, acc, z_buf, full, nw,
    in_sem, out_sem, pair_s, pair_r, xy_s, xy_r, zr_s, zr_r, zg_s, zg_r,
    ag_s, ag_r, to_s, to_r,
):
    frames, ch, dp, rep, rows, transposed, parts = plan
    chips = dp // 2
    lin = rows * ch // LANES
    part = lin // parts
    me = lax.axis_index("dp")
    z = lax.axis_index("rep")
    core = me % 2
    g = me // 2
    partner = g * 2 + 1 - core

    loads = [
        pltpu.make_async_copy(s, d, in_sem.at[i])
        for i, (s, d) in enumerate(
            [(clip_hbm, clip), (w_hbm, w_lin), (cot_hbm, cot), (ma_hbm, ma), (m1_hbm, m1), (m2_hbm, m2)]
        )
    ]
    for c in loads:
        c.start()

    barrier = pltpu.get_barrier_semaphore()
    pl.semaphore_signal(barrier, inc=1, device_id={"dp": partner})
    for k in range(1, chips):
        pl.semaphore_signal(barrier, inc=1, device_id={"dp": (g + k) % chips * 2 + core})
    for k in range(1, rep):
        pl.semaphore_signal(barrier, inc=1, device_id={"rep": (z + k) % rep})

    reach = DILATION * (TAPS // 2)
    base = 16
    split = TAPS * ch

    loads[0].wait()
    for h in range(ch // LANES):
        cols = slice(h * LANES, (h + 1) * LANES)
        a0 = alpha_ref[0:1, cols]
        v = clip[:, cols].astype(jnp.float32)
        r = reduced(a0 * v)
        s = sin_of(r, r * r)
        padded[h, 0:base, :] = jnp.zeros((base, LANES), jnp.float32)
        padded[h, base + frames : base + frames + base, :] = jnp.zeros((base, LANES), jnp.float32)
        padded[h, base : base + frames, :] = v + s * s * (1.0 / a0)
    for k in range(TAPS):
        for h in range(ch // LANES):
            start = base + DILATION * k - reach
            win[:, k * ch + h * LANES : k * ch + (h + 1) * LANES] = padded[
                h, start : start + frames, :
            ].astype(jnp.bfloat16)

    loads[1].wait()
    w32[...] = w_lin[...].astype(jnp.float32)
    per = ch // LANES
    for h in range(per):
        w_mat[:, h * LANES : (h + 1) * LANES] = w32[pl.ds(h, split + ch, stride=per), :].astype(jnp.bfloat16)

    loads[2].wait()
    lhs[1] = cot[...].astype(jnp.float32).T.astype(jnp.bfloat16)

    a1 = alpha_ref[1:2, :]
    inv1 = 1.0 / a1
    chunk = 256

    def forward(c, carry):
        at = pl.ds(pl.multiple_of(c * chunk, chunk), chunk)
        hidden = dot(win[at, :split], w_mat[:split, :], ((1,), (0,)))
        back = dot(cot[at, :], w_mat[split:, :], ((1,), (1,)))
        r = reduced(a1 * hidden)
        r2 = r * r
        s = sin_of(r, r2)
        win[at, split : split + ch] = (hidden + s * s * inv1).astype(jnp.bfloat16)
        d_hidden = back * (1.0 + 2.0 * s * cos_of(r2))
        lhs[0, :, at] = d_hidden.astype(jnp.bfloat16).astype(jnp.float32).T.astype(jnp.bfloat16)
        return carry

    lax.fori_loop(0, frames // chunk, forward, 0)

    def block(b):
        return grad.at[pl.ds(pl.multiple_of(b * rows, rows), rows), :]

    def tile(t):
        side = t // TAPS
        part_of = win[:, pl.ds(pl.multiple_of(t * ch, ch), ch)]
        if transposed:
            value = dot(lhs[side], part_of, ((1,), (0,)))
        else:
            value = dot(lhs[side], part_of, ((1,), (0,))).T
        grad[pl.ds(pl.multiple_of(t * ch, ch), ch), :] = value

    if not transposed:
        lax.fori_loop(0, TAPS, lambda t, c: (tile(t), c)[1], 0)
        second = dot(lhs[1], win[:, split : split + ch], ((1,), (0,)))
        grad[split : split + ch, :] = second.T

    pl.semaphore_wait(barrier, chips + rep - 1)

    def chip_at(o):
        return (g + 1 + o) % chips

    def pair_copy(o):
        return pltpu.make_async_remote_copy(
            block(chip_at(o) * 2 + 1 - core), pair_buf.at[o], pair_s.at[o], pair_r.at[o],
            device_id={"dp": partner},
        )

    def xy_copy(o):
        to = chip_at(o)
        return pltpu.make_async_remote_copy(
            block(to * 2 + core), xy_buf.at[o], xy_s.at[o], xy_r.at[o],
            device_id={"dp": to * 2 + core},
        )

    def produce(o, carry):
        i = chip_at(o)
        if transposed:
            tile(i * 2 + 1 - core)
        pair_copy(o).start()
        if transposed:
            tile(i * 2 + core)
        return carry

    lax.fori_loop(0, chips, produce, 0)

    def add_pair(o):
        pair_copy(o).wait_recv()
        b = chip_at(o) * 2 + core
        at = pl.ds(pl.multiple_of(b * rows, rows), rows)
        grad[at, :] = grad[at, :] + pair_buf[o]

    def send_on(o, carry):
        add_pair(o)
        xy_copy(o).start()
        return carry

    lax.fori_loop(0, chips - 1, send_on, 0)
    add_pair(chips - 1)

    def add_chip(o, total):
        xy_copy(o).wait_recv()
        return total + xy_buf[o]

    total = lax.fori_loop(
        0, chips - 1, add_chip, grad[pl.ds(pl.multiple_of(me * rows, rows), rows), :]
    )
    if transposed:
        total = total.T
    for h in range(per):
        acc[pl.ds(h, rows, stride=per), :] = total[:, h * LANES : (h + 1) * LANES]

    def z_peer(k):
        return (z + k) % rep

    def part_at(q):
        return pl.ds(pl.multiple_of(q * part, part), part)

    def zr_copy(k):
        src = acc.at[part_at(z_peer(k))] if parts > 1 else acc
        return pltpu.make_async_remote_copy(
            src, z_buf.at[k - 1 if parts > 1 else z], zr_s.at[k - 1], zr_r.at[k - 1],
            device_id={"rep": z_peer(k)},
        )

    def zr_wait(k):
        return pltpu.make_async_remote_copy(
            acc.at[part_at(0)] if parts > 1 else acc,
            z_buf.at[k - 1 if parts > 1 else (z + rep - k) % rep], zr_s.at[k - 1], zr_r.at[k - 1],
            device_id={"rep": z_peer(k)},
        )

    def zg_copy(k):
        at = part_at(z)
        return pltpu.make_async_remote_copy(
            full.at[at], full.at[at], zg_s.at[k - 1], zg_r.at[k - 1], device_id={"rep": z_peer(k)},
        )

    def zg_wait(k):
        at = part_at((z + rep - k) % rep)
        return pltpu.make_async_remote_copy(
            full.at[at], full.at[at], zg_s.at[k - 1], zg_r.at[k - 1], device_id={"rep": z_peer(k)},
        )

    for k in range(1, rep):
        zr_copy(k).start()
    if parts > 1:
        own = acc[part_at(z), :]
        for k in range(1, rep):
            zr_wait(k).wait_recv()
            own = own + z_buf[k - 1]
        full[part_at(z), :] = own
        for k in range(1, rep):
            zg_copy(k).start()
    else:
        z_buf[z] = acc[...]
        for k in range(1, rep):
            zr_wait(k).wait_recv()
        own = z_buf[0]
        for k in range(1, rep):
            own = own + z_buf[k]
        full[...] = own

    for c in loads[3:]:
        c.wait()

    def part_of(k):
        return (z + parts - k) % parts if parts > 1 else 0

    def place(owner, k):
        return ow_hbm.at[pl.ds(pl.multiple_of(owner * lin + part_of(k) * part, part), part), :]

    def outs(k):
        at = part_at(part_of(k))
        return [
            pltpu.make_async_copy(nw.at[at], place(me, k), out_sem.at[k, 0]),
            pltpu.make_async_copy(ma.at[at], oma_hbm.at[at], out_sem.at[k, 1]),
            pltpu.make_async_copy(m1.at[at], om1_hbm.at[at], out_sem.at[k, 2]),
            pltpu.make_async_copy(m2.at[at], om2_hbm.at[at], out_sem.at[k, 3]),
        ]

    def ag_copy(k, j):
        return pltpu.make_async_remote_copy(
            nw.at[part_at(part_of(k))], place(me, k), ag_s.at[k, j], ag_r.at[k, j],
            device_id={"dp": (g + j) % chips * 2 + core},
        )

    def ag_wait(k, j):
        at = place((g + chips - j) % chips * 2 + core, k)
        return pltpu.make_async_remote_copy(
            at, at, ag_s.at[k, j], ag_r.at[k, j], device_id={"dp": (g + j) % chips * 2 + core},
        )

    def to_copy(k, j):
        at = place((g + chips - j) % chips * 2 + core, k)
        src = nw.at[part_at(part_of(k))] if isinstance(j, int) and j == 0 else at
        return pltpu.make_async_remote_copy(
            src, at, to_s.at[k, j], to_r.at[k, j], device_id={"dp": partner},
        )

    def to_wait(k, j):
        at = place((g + chips - j) % chips * 2 + 1 - core, k)
        return pltpu.make_async_remote_copy(
            at, at, to_s.at[k, j], to_r.at[k, j], device_id={"dp": partner},
        )

    def loop(lo, hi, f):
        lax.fori_loop(lo, hi, lambda j, c: (f(j), c)[1], 0)

    for k in range(parts):
        if k > 0:
            zg_wait(k).wait_recv()
        at = part_at(part_of(k))
        new_master, new_first, new_second = adam(full[at, :], ma[at, :], m1[at, :], m2[at, :])
        nw[at, :] = new_master.astype(jnp.bfloat16)
        loop(1, chips, lambda j: ag_copy(k, j).start())
        to_copy(k, 0).start()
        ma[at, :] = new_master
        m1[at, :] = new_first
        m2[at, :] = new_second
        for c in outs(k):
            c.start()

    for k in range(parts):

        def hand_on(j):
            ag_wait(k, j).wait_recv()
            to_copy(k, j).start()

        loop(1, chips, hand_on)

    for k in range(parts):
        loop(0, chips, lambda j: to_wait(k, j).wait_recv())

    loop(0, chips, lambda o: pair_copy(o).wait_send())
    loop(0, chips - 1, lambda o: xy_copy(o).wait_send())
    for k in range(1, rep):
        zr_copy(k).wait_send()
        if parts > 1:
            zg_copy(k).wait_send()
    for k in range(parts):
        loop(1, chips, lambda j: ag_copy(k, j).wait_send())
        to_copy(k, 0).wait_send()
        loop(1, chips, lambda j: to_copy(k, j).wait_send())
        for c in outs(k):
            c.wait()


def shards(dp, rep, clips, cotangent, alphas, weights, master, first_moment, second_moment):
    frames, ch = clips.shape[1:]
    params = weights.shape[0]
    own = master.shape[0]
    rows = own // ch
    lin = own // LANES
    parts = rep if lin % (16 * rep) == 0 else 1
    part = lin // parts
    chips = dp // 2
    transposed = rows == ch
    plan = (frames, ch, dp, rep, rows, transposed, parts)
    anywhere = pl.BlockSpec(memory_space=pl.ANY)
    f32, bf16 = jnp.float32, jnp.bfloat16
    dma = pltpu.SemaphoreType.DMA
    outs = pl.pallas_call(
        functools.partial(step_kernel, plan),
        out_shape=(
            jax.ShapeDtypeStruct((params // LANES, LANES), bf16),
            jax.ShapeDtypeStruct((lin, LANES), f32),
            jax.ShapeDtypeStruct((lin, LANES), f32),
            jax.ShapeDtypeStruct((lin, LANES), f32),
        ),
        in_specs=[anywhere, anywhere, pl.BlockSpec(memory_space=pltpu.VMEM)] + [anywhere] * 4,
        out_specs=(anywhere,) * 4,
        scratch_shapes=[
            pltpu.VMEM((frames, ch), bf16),
            pltpu.VMEM((frames, ch), bf16),
            pltpu.VMEM((params // LANES, LANES), bf16),
            pltpu.VMEM((params // LANES, LANES), f32),
            pltpu.VMEM((params // ch, ch), bf16),
            pltpu.VMEM((lin, LANES), f32),
            pltpu.VMEM((lin, LANES), f32),
            pltpu.VMEM((lin, LANES), f32),
            pltpu.VMEM((ch // LANES, frames + 32, LANES), f32),
            pltpu.VMEM((frames, (TAPS + 1) * ch), bf16),
            pltpu.VMEM((2, ch, frames), bf16),
            pltpu.VMEM((params // ch, ch), f32),
            pltpu.VMEM((chips, rows, ch), f32),
            pltpu.VMEM((chips - 1, rows, ch), f32),
            pltpu.VMEM((lin, LANES), f32),
            pltpu.VMEM((rep, part, LANES), f32),
            pltpu.VMEM((lin, LANES), f32),
            pltpu.VMEM((lin, LANES), bf16),
            dma((6,)),
            dma((parts, 4)),
            dma((chips,)), dma((chips,)),
            dma((chips,)), dma((chips,)),
            dma((rep,)), dma((rep,)),
            dma((rep,)), dma((rep,)),
            dma((parts, chips)), dma((parts, chips)),
            dma((parts, chips)), dma((parts, chips)),
        ],
        compiler_params=pltpu.CompilerParams(
            collective_id=0, has_side_effects=True, vmem_limit_bytes=48 * 1024 * 1024
        ),
        name="train_step",
    )(
        clips[0],
        cotangent[0],
        alphas,
        weights.reshape(params // LANES, LANES),
        master.reshape(lin, LANES),
        first_moment.reshape(lin, LANES),
        second_moment.reshape(lin, LANES),
    )
    return tuple(o.reshape(-1) for o in outs)


def solution(mesh):
    return jax.shard_map(
        functools.partial(shards, mesh.shape["dp"], mesh.shape["rep"]),
        mesh=mesh,
        in_specs=(
            P(("dp", "rep"), None, None),
            P(("dp", "rep"), None, None),
            P(),
            P(),
            P("dp"),
            P("dp"),
            P("dp"),
        ),
        out_specs=(P(), P("dp"), P("dp"), P("dp")),
        check_vma=False,
    )
```

```python
import functools

import jax
import jax.numpy as jnp
from jax import lax
from jax.experimental import pallas as pl
from jax.experimental.pallas import tpu as pltpu
from jax.sharding import PartitionSpec as P

TAPS = 7
DILATION = 3
LANES = 128
PIECES = 2

BIAS_ONE = 0.9999734386011124
BIAS_TWO = 0.09520785288629041

PI_A = 3.140625
PI_B = 9.67502593994140625e-4
PI_C = 1.509957990978376432e-7
INV_PI = 0.3183098861837907

SIN = (-0.16666659712791443, 0.008333083242177963, -0.00019810810044873506, 2.6083068860316416e-06)
COS = (-0.5, 0.04166664183139801, -0.001388839678838849, 2.4761575332377106e-05, -2.607200428883516e-07)


def reduced(u):
    k = jnp.round(u * INV_PI)
    return ((u - k * PI_A) - k * PI_B) - k * PI_C


def sin_of(r, r2):
    return r + r * (r2 * (SIN[0] + r2 * (SIN[1] + r2 * (SIN[2] + r2 * SIN[3]))))


def cos_of(r2):
    return 1.0 + r2 * (COS[0] + r2 * (COS[1] + r2 * (COS[2] + r2 * (COS[3] + r2 * COS[4]))))


def dot(a, b, dims):
    return lax.dot_general(a, b, (dims, ((), ())), preferred_element_type=jnp.float32)


def adam(gradient, master, first_moment, second_moment):
    new_first = 0.9 * first_moment + 0.1 * gradient
    new_second = 0.999 * second_moment + 0.001 * gradient * gradient
    new_master = master - 0.001 * (new_first / BIAS_ONE) / (jnp.sqrt(new_second / BIAS_TWO) + 1e-08)
    return new_master, new_first, new_second


def step_kernel(
    plan,
    clip_hbm, cot_hbm, alpha_hbm, w_hbm, ma_hbm, m1_hbm, m2_hbm,
    ow_hbm, oma_hbm, om1_hbm, om2_hbm,
    clip, cot, alpha_ref, w_lin, w32, w_mat, ma, m1, m2,
    padded, win, lhs, grad, pair_buf, xy_buf, acc, z_buf, full, nw,
    in_sem, out_sem, pair_s, pair_r, xy_s, xy_r, zr_s, zr_r, zg_s, zg_r,
    ag_s, ag_r, to_s, to_r,
):
    frames, ch, dp, rep, rows, transposed, chunks, parts = plan
    chips = dp // 2
    lin = rows * ch // LANES
    chunk_lin = lin // chunks
    part = chunk_lin // parts
    wide = ch // chunks
    me = lax.axis_index("dp")
    z = lax.axis_index("rep")
    core = me % 2
    g = me // 2
    partner = g * 2 + 1 - core

    loads = [
        pltpu.make_async_copy(s, d, in_sem.at[i])
        for i, (s, d) in enumerate(
            [(alpha_hbm, alpha_ref), (clip_hbm, clip), (w_hbm, w_lin), (cot_hbm, cot), (ma_hbm, ma), (m1_hbm, m1), (m2_hbm, m2)]
        )
    ]
    for c in loads:
        c.start()

    barrier = pltpu.get_barrier_semaphore()
    pl.semaphore_signal(barrier, inc=1, device_id={"dp": partner})
    for k in range(1, chips):
        pl.semaphore_signal(barrier, inc=1, device_id={"dp": (g + k) % chips * 2 + core})
    for k in range(1, rep):
        pl.semaphore_signal(barrier, inc=1, device_id={"rep": (z + k) % rep})

    reach = DILATION * (TAPS // 2)
    base = 16
    split = TAPS * ch

    loads[0].wait()
    loads[1].wait()
    for h in range(ch // LANES):
        cols = slice(h * LANES, (h + 1) * LANES)
        a0 = alpha_ref[0:1, cols]
        v = clip[:, cols].astype(jnp.float32)
        r = reduced(a0 * v)
        s = sin_of(r, r * r)
        padded[h, 0:base, :] = jnp.zeros((base, LANES), jnp.float32)
        padded[h, base + frames : base + frames + base, :] = jnp.zeros((base, LANES), jnp.float32)
        padded[h, base : base + frames, :] = v + s * s * (1.0 / a0)
    for k in range(TAPS):
        for h in range(ch // LANES):
            start = base + DILATION * k - reach
            win[:, k * ch + h * LANES : k * ch + (h + 1) * LANES] = padded[
                h, start : start + frames, :
            ].astype(jnp.bfloat16)

    loads[2].wait()
    w32[...] = w_lin[...].astype(jnp.float32)
    per = ch // LANES
    for h in range(per):
        w_mat[:, h * LANES : (h + 1) * LANES] = w32[pl.ds(h, split + ch, stride=per), :].astype(jnp.bfloat16)

    loads[3].wait()
    lhs[1] = cot[...].T

    a1 = alpha_ref[1:2, :]
    inv1 = 1.0 / a1
    chunk = 256

    def forward(c, carry):
        at = pl.ds(pl.multiple_of(c * chunk, chunk), chunk)
        hidden = dot(win[at, :split], w_mat[:split, :], ((1,), (0,)))
        back = dot(cot[at, :], w_mat[split:, :], ((1,), (1,)))
        r = reduced(a1 * hidden)
        r2 = r * r
        s = sin_of(r, r2)
        win[at, split : split + ch] = (hidden + s * s * inv1).astype(jnp.bfloat16)
        d_hidden = back * (1.0 + 2.0 * s * cos_of(r2))
        lhs[0, :, at] = d_hidden.astype(jnp.bfloat16).T
        return carry

    lax.fori_loop(0, frames // chunk, forward, 0)

    def block(b):
        return grad.at[pl.ds(pl.multiple_of(b * rows, rows), rows), :]

    def tile(t):
        side = t // TAPS
        part_of = win[:, pl.ds(pl.multiple_of(t * ch, ch), ch)]
        if transposed:
            value = dot(lhs[side], part_of, ((1,), (0,)))
        else:
            value = dot(lhs[side], part_of, ((1,), (0,))).T
        grad[pl.ds(pl.multiple_of(t * ch, ch), ch), :] = value

    if not transposed:
        lax.fori_loop(0, TAPS, lambda t, c: (tile(t), c)[1], 0)
        second = dot(lhs[1], win[:, split : split + ch], ((1,), (0,)))
        grad[split : split + ch, :] = second.T

    pl.semaphore_wait(barrier, chips + rep - 1)

    def chip_at(o):
        return (g + 1 + o) % chips

    def pair_copy(o):
        return pltpu.make_async_remote_copy(
            block(chip_at(o) * 2 + 1 - core), pair_buf.at[o], pair_s.at[o], pair_r.at[o],
            device_id={"dp": partner},
        )

    def xy_copy(s, o):
        to = chip_at(o)
        return pltpu.make_async_remote_copy(
            block(to * 2 + core).at[:, s * wide : (s + 1) * wide], xy_buf.at[s, o], xy_s.at[s, o], xy_r.at[s, o],
            device_id={"dp": to * 2 + core},
        )

    def produce(o, carry):
        i = chip_at(o)
        if transposed:
            tile(i * 2 + 1 - core)
        pair_copy(o).start()
        if transposed:
            tile(i * 2 + core)
        return carry

    lax.fori_loop(0, chips, produce, 0)

    def add_pair(o):
        pair_copy(o).wait_recv()
        b = chip_at(o) * 2 + core
        at = pl.ds(pl.multiple_of(b * rows, rows), rows)
        grad[at, :] = grad[at, :] + pair_buf[o]

    def loop(lo, hi, f):
        lax.fori_loop(lo, hi, lambda j, c: (f(j), c)[1], 0)

    def send_on(o):
        add_pair(o)
        xy_copy(0, o).start()

    def z_peer(k):
        return (z + k) % rep

    def part_at(s, q):
        return pl.ds(pl.multiple_of(s * chunk_lin + q * part, part), part)

    def zr_copy(s, k, wait=False):
        if parts > 1:
            src, slot = acc.at[part_at(s, z_peer(k))], k - 1
        else:
            src, slot = acc.at[part_at(s, 0)], (z + rep - k) % rep if wait else z
        return pltpu.make_async_remote_copy(
            src, z_buf.at[s, slot], zr_s.at[s, k - 1], zr_r.at[s, k - 1], device_id={"rep": z_peer(k)},
        )

    def zg_copy(s, k, wait=False):
        at = part_at(s, (z + rep - k) % rep if wait else z)
        return pltpu.make_async_remote_copy(
            full.at[at], full.at[at], zg_s.at[s, k - 1], zg_r.at[s, k - 1], device_id={"rep": z_peer(k)},
        )

    def sum_chips(s):
        def add_chip(o, total):
            xy_copy(s, o).wait_recv()
            return total + xy_buf[s, o]

        at = pl.ds(pl.multiple_of(me * rows, rows), rows)
        total = lax.fori_loop(0, chips - 1, add_chip, grad[at, s * wide : (s + 1) * wide])
        if transposed:
            total = total.T
        for h in range(per):
            acc[pl.ds(s * chunk_lin + h, chunk_lin // per, stride=per), :] = total[:, h * LANES : (h + 1) * LANES]
        for k in range(1, rep):
            zr_copy(s, k).start()

    def sum_replicas(s):
        if parts > 1:
            own = acc[part_at(s, z), :]
            for k in range(1, rep):
                zr_copy(s, k, True).wait_recv()
                own = own + z_buf[s, k - 1]
            full[part_at(s, z), :] = own
            for k in range(1, rep):
                zg_copy(s, k).start()
        else:
            z_buf[s, z] = acc[part_at(s, 0), :]
            for k in range(1, rep):
                zr_copy(s, k, True).wait_recv()
            own = z_buf[s, 0]
            for k in range(1, rep):
                own = own + z_buf[s, k]
            full[part_at(s, 0), :] = own

    def part_of(s, k):
        return part_at(s, (z + parts - k) % parts if parts > 1 else 0)

    def place(owner, s, k):
        q = (z + parts - k) % parts if parts > 1 else 0
        return ow_hbm.at[pl.ds(pl.multiple_of(owner * lin + s * chunk_lin + q * part, part), part), :]

    def outs(s, k):
        at = part_of(s, k)
        return [
            pltpu.make_async_copy(nw.at[at], place(me, s, k), out_sem.at[s, k, 0]),
            pltpu.make_async_copy(ma.at[at], oma_hbm.at[at], out_sem.at[s, k, 1]),
            pltpu.make_async_copy(m1.at[at], om1_hbm.at[at], out_sem.at[s, k, 2]),
            pltpu.make_async_copy(m2.at[at], om2_hbm.at[at], out_sem.at[s, k, 3]),
        ]

    def ag_copy(s, k, j, wait=False):
        if wait:
            src = dst = place((g + chips - j) % chips * 2 + core, s, k)
        else:
            src, dst = nw.at[part_of(s, k)], place(me, s, k)
        return pltpu.make_async_remote_copy(
            src, dst, ag_s.at[s, k, j], ag_r.at[s, k, j], device_id={"dp": (g + j) % chips * 2 + core},
        )

    def to_copy(s, k, j):
        at = place((g + chips - j) % chips * 2 + core, s, k)
        src = nw.at[part_of(s, k)] if isinstance(j, int) and j == 0 else at
        return pltpu.make_async_remote_copy(
            src, at, to_s.at[s, k, j], to_r.at[s, k, j], device_id={"dp": partner},
        )

    def to_wait(s, k, j):
        at = place((g + chips - j) % chips * 2 + 1 - core, s, k)
        return pltpu.make_async_remote_copy(
            at, at, to_s.at[s, k, j], to_r.at[s, k, j], device_id={"dp": partner},
        )

    def update(s, k):
        if k > 0:
            zg_copy(s, k, True).wait_recv()
        at = part_of(s, k)
        new_master, new_first, new_second = adam(full[at, :], ma[at, :], m1[at, :], m2[at, :])
        nw[at, :] = new_master.astype(jnp.bfloat16)
        loop(1, chips, lambda j: ag_copy(s, k, j).start())
        to_copy(s, k, 0).start()
        ma[at, :] = new_master
        m1[at, :] = new_first
        m2[at, :] = new_second
        for c in outs(s, k):
            c.start()

    def hand_on(s, k):
        def one(j):
            ag_copy(s, k, j, True).wait_recv()
            to_copy(s, k, j).start()

        loop(1, chips, one)

    loop(0, chips - 1, send_on)
    add_pair(chips - 1)
    for s in range(1, chunks):
        loop(0, chips - 1, lambda o: xy_copy(s, o).start())
    for c in loads[4:]:
        c.wait()

    sum_chips(0)
    sum_replicas(0)
    update(0, 0)
    for s in range(1, chunks):
        sum_chips(s)
        for k in range(1, parts):
            update(s - 1, k)
        sum_replicas(s)
        update(s, 0)
        for k in range(parts):
            hand_on(s - 1, k)
    for k in range(1, parts):
        update(chunks - 1, k)
    for k in range(parts):
        hand_on(chunks - 1, k)

    for s in range(chunks):
        for k in range(parts):
            loop(0, chips, lambda j: to_wait(s, k, j).wait_recv())

    loop(0, chips, lambda o: pair_copy(o).wait_send())
    for s in range(chunks):
        loop(0, chips - 1, lambda o: xy_copy(s, o).wait_send())
        for k in range(1, rep):
            zr_copy(s, k).wait_send()
            if parts > 1:
                zg_copy(s, k).wait_send()
        for k in range(parts):
            loop(1, chips, lambda j: ag_copy(s, k, j).wait_send())
            to_copy(s, k, 0).wait_send()
            loop(1, chips, lambda j: to_copy(s, k, j).wait_send())
            for c in outs(s, k):
                c.wait()


def results_kernel(*refs):
    half = len(refs) // 2
    sem = refs[-1]
    copies = []
    for i, (src, dst) in enumerate(zip(refs[:half], refs[half:-1])):
        n = src.shape[0] // PIECES
        for p in range(PIECES):
            at = pl.ds(p * n, n)
            copies.append(pltpu.make_async_copy(src.at[at], dst.at[at], sem.at[i, p]))
    for c in copies:
        c.start()
    for c in copies:
        c.wait()


def shards(dp, rep, clips, cotangent, alphas, weights, master, first_moment, second_moment):
    frames, ch = clips.shape[1:]
    params = weights.shape[0]
    own = master.shape[0]
    rows = own // ch
    lin = own // LANES
    chips = dp // 2
    transposed = rows == ch
    chunks = ch // LANES if transposed else 1
    parts = rep if lin // chunks % (16 * rep) == 0 else 1
    part = lin // chunks // parts
    plan = (frames, ch, dp, rep, rows, transposed, chunks, parts)
    anywhere = pl.BlockSpec(memory_space=pl.ANY)
    f32, bf16 = jnp.float32, jnp.bfloat16
    dma = pltpu.SemaphoreType.DMA
    outs = pl.pallas_call(
        functools.partial(step_kernel, plan),
        out_shape=(
            jax.ShapeDtypeStruct((params // LANES, LANES), bf16),
            jax.ShapeDtypeStruct((lin, LANES), f32),
            jax.ShapeDtypeStruct((lin, LANES), f32),
            jax.ShapeDtypeStruct((lin, LANES), f32),
        ),
        in_specs=[anywhere] * 7,
        out_specs=(anywhere,) * 4,
        scratch_shapes=[
            pltpu.VMEM((frames, ch), bf16),
            pltpu.VMEM((frames, ch), bf16),
            pltpu.VMEM(alphas.shape, f32),
            pltpu.VMEM((params // LANES, LANES), bf16),
            pltpu.VMEM((params // LANES, LANES), f32),
            pltpu.VMEM((params // ch, ch), bf16),
            pltpu.VMEM((lin, LANES), f32),
            pltpu.VMEM((lin, LANES), f32),
            pltpu.VMEM((lin, LANES), f32),
            pltpu.VMEM((ch // LANES, frames + 32, LANES), f32),
            pltpu.VMEM((frames, (TAPS + 1) * ch), bf16),
            pltpu.VMEM((2, ch, frames), bf16),
            pltpu.VMEM((params // ch, ch), f32),
            pltpu.VMEM((chips, rows, ch), f32),
            pltpu.VMEM((chunks, chips - 1, rows, ch // chunks), f32),
            pltpu.VMEM((lin, LANES), f32),
            pltpu.VMEM((chunks, rep, part, LANES), f32),
            pltpu.VMEM((lin, LANES), f32),
            pltpu.VMEM((lin, LANES), bf16),
            dma((7,)),
            dma((chunks, parts, 4)),
            dma((chips,)), dma((chips,)),
            dma((chunks, chips)), dma((chunks, chips)),
            dma((chunks, rep)), dma((chunks, rep)),
            dma((chunks, rep)), dma((chunks, rep)),
            dma((chunks, parts, chips)), dma((chunks, parts, chips)),
            dma((chunks, parts, chips)), dma((chunks, parts, chips)),
        ],
        compiler_params=pltpu.CompilerParams(
            collective_id=0, has_side_effects=True, vmem_limit_bytes=64 * 1024 * 1024
        ),
        name="train_step",
    )(
        clips[0],
        cotangent[0],
        alphas,
        weights.reshape(params // LANES, LANES),
        master.reshape(lin, LANES),
        first_moment.reshape(lin, LANES),
        second_moment.reshape(lin, LANES),
    )
    outs = pl.pallas_call(
        results_kernel,
        out_shape=tuple(jax.ShapeDtypeStruct(o.shape, o.dtype) for o in outs),
        in_specs=[anywhere] * len(outs),
        out_specs=(anywhere,) * len(outs),
        scratch_shapes=[dma((len(outs), PIECES))],
        compiler_params=pltpu.CompilerParams(vmem_limit_bytes=64 * 1024 * 1024),
        name="results",
    )(*outs)
    return tuple(o.reshape(-1) for o in outs)


def solution(mesh):
    return jax.shard_map(
        functools.partial(shards, mesh.shape["dp"], mesh.shape["rep"]),
        mesh=mesh,
        in_specs=(
            P(("dp", "rep"), None, None),
            P(("dp", "rep"), None, None),
            P(),
            P(),
            P("dp"),
            P("dp"),
            P("dp"),
        ),
        out_specs=(P(), P("dp"), P("dp"), P("dp")),
        check_vma=False,
    )
```

```python
import functools

import jax
import jax.numpy as jnp
from jax import lax
from jax.experimental import pallas as pl
from jax.experimental.pallas import tpu as pltpu
from jax.sharding import PartitionSpec as P

TAPS = 7
DILATION = 3
LANES = 128
PIECES = 2

BIAS_ONE = 0.9999734386011124
BIAS_TWO = 0.09520785288629041

PI_A = 3.140625
PI_B = 9.67502593994140625e-4
PI_C = 1.509957990978376432e-7
INV_PI = 0.3183098861837907

SIN = (-0.16666659712791443, 0.008333083242177963, -0.00019810810044873506, 2.6083068860316416e-06)
COS = (-0.5, 0.04166664183139801, -0.001388839678838849, 2.4761575332377106e-05, -2.607200428883516e-07)


def reduced(u):
    k = jnp.round(u * INV_PI)
    return ((u - k * PI_A) - k * PI_B) - k * PI_C


def sin_of(r, r2):
    return r + r * (r2 * (SIN[0] + r2 * (SIN[1] + r2 * (SIN[2] + r2 * SIN[3]))))


def cos_of(r2):
    return 1.0 + r2 * (COS[0] + r2 * (COS[1] + r2 * (COS[2] + r2 * (COS[3] + r2 * COS[4]))))


def dot(a, b, dims):
    return lax.dot_general(a, b, (dims, ((), ())), preferred_element_type=jnp.float32)


def adam(gradient, master, first_moment, second_moment):
    new_first = 0.9 * first_moment + 0.1 * gradient
    new_second = 0.999 * second_moment + 0.001 * gradient * gradient
    new_master = master - 0.001 * (new_first / BIAS_ONE) / (jnp.sqrt(new_second / BIAS_TWO) + 1e-08)
    return new_master, new_first, new_second


def step_kernel(
    plan,
    clip_hbm, cot_hbm, alpha_hbm, w_hbm, ma_hbm, m1_hbm, m2_hbm,
    ow_hbm, oma_hbm, om1_hbm, om2_hbm,
    clip, cot, alpha_ref, w_lin, w32, w_mat, ma, m1, m2,
    padded, win, lhs, grad, pair_buf, xy_buf, acc, z_buf, full, ow, oma, om1, om2,
    in_sem, out_sem, ow_sem, pair_s, pair_r, xy_s, xy_r, zr_s, zr_r, zg_s, zg_r,
    ag_s, ag_r, to_s, to_r,
):
    frames, ch, dp, rep, rows, transposed, chunks, parts = plan
    chips = dp // 2
    lin = rows * ch // LANES
    chunk_lin = lin // chunks
    part = chunk_lin // parts
    wide = ch // chunks
    me = lax.axis_index("dp")
    z = lax.axis_index("rep")
    core = me % 2
    g = me // 2
    partner = g * 2 + 1 - core

    loads = [
        pltpu.make_async_copy(s, d, in_sem.at[i])
        for i, (s, d) in enumerate(
            [(alpha_hbm, alpha_ref), (clip_hbm, clip), (w_hbm, w_lin), (cot_hbm, cot), (ma_hbm, ma), (m1_hbm, m1), (m2_hbm, m2)]
        )
    ]
    for c in loads:
        c.start()

    barrier = pltpu.get_barrier_semaphore()
    pl.semaphore_signal(barrier, inc=1, device_id={"dp": partner})
    for k in range(1, chips):
        pl.semaphore_signal(barrier, inc=1, device_id={"dp": (g + k) % chips * 2 + core})
    for k in range(1, rep):
        pl.semaphore_signal(barrier, inc=1, device_id={"rep": (z + k) % rep})

    reach = DILATION * (TAPS // 2)
    base = 16
    split = TAPS * ch

    loads[0].wait()
    loads[1].wait()
    for h in range(ch // LANES):
        cols = slice(h * LANES, (h + 1) * LANES)
        a0 = alpha_ref[0:1, cols]
        v = clip[:, cols].astype(jnp.float32)
        r = reduced(a0 * v)
        s = sin_of(r, r * r)
        padded[h, 0:base, :] = jnp.zeros((base, LANES), jnp.float32)
        padded[h, base + frames : base + frames + base, :] = jnp.zeros((base, LANES), jnp.float32)
        padded[h, base : base + frames, :] = v + s * s * (1.0 / a0)
    for k in range(TAPS):
        for h in range(ch // LANES):
            start = base + DILATION * k - reach
            win[:, k * ch + h * LANES : k * ch + (h + 1) * LANES] = padded[
                h, start : start + frames, :
            ].astype(jnp.bfloat16)

    loads[2].wait()
    w32[...] = w_lin[...].astype(jnp.float32)
    per = ch // LANES
    for h in range(per):
        w_mat[:, h * LANES : (h + 1) * LANES] = w32[pl.ds(h, split + ch, stride=per), :].astype(jnp.bfloat16)

    loads[3].wait()
    lhs[1] = cot[...].T

    a1 = alpha_ref[1:2, :]
    inv1 = 1.0 / a1
    chunk = 256

    def forward(c, carry):
        at = pl.ds(pl.multiple_of(c * chunk, chunk), chunk)
        hidden = dot(win[at, :split], w_mat[:split, :], ((1,), (0,)))
        back = dot(cot[at, :], w_mat[split:, :], ((1,), (1,)))
        r = reduced(a1 * hidden)
        r2 = r * r
        s = sin_of(r, r2)
        win[at, split : split + ch] = (hidden + s * s * inv1).astype(jnp.bfloat16)
        d_hidden = back * (1.0 + 2.0 * s * cos_of(r2))
        lhs[0, :, at] = d_hidden.astype(jnp.bfloat16).T
        return carry

    lax.fori_loop(0, frames // chunk, forward, 0)

    def block(b):
        return grad.at[pl.ds(pl.multiple_of(b * rows, rows), rows), :]

    def tile(t):
        side = t // TAPS
        part_of = win[:, pl.ds(pl.multiple_of(t * ch, ch), ch)]
        if transposed:
            value = dot(lhs[side], part_of, ((1,), (0,)))
        else:
            value = dot(lhs[side], part_of, ((1,), (0,))).T
        grad[pl.ds(pl.multiple_of(t * ch, ch), ch), :] = value

    if not transposed:
        lax.fori_loop(0, TAPS, lambda t, c: (tile(t), c)[1], 0)
        second = dot(lhs[1], win[:, split : split + ch], ((1,), (0,)))
        grad[split : split + ch, :] = second.T

    pl.semaphore_wait(barrier, chips + rep - 1)

    def chip_at(o):
        return (g + 1 + o) % chips

    def pair_copy(o):
        return pltpu.make_async_remote_copy(
            block(chip_at(o) * 2 + 1 - core), pair_buf.at[o], pair_s.at[o], pair_r.at[o],
            device_id={"dp": partner},
        )

    def xy_copy(s, o):
        to = chip_at(o)
        return pltpu.make_async_remote_copy(
            block(to * 2 + core).at[:, s * wide : (s + 1) * wide], xy_buf.at[s, o], xy_s.at[s, o], xy_r.at[s, o],
            device_id={"dp": to * 2 + core},
        )

    def produce(o, carry):
        i = chip_at(o)
        if transposed:
            tile(i * 2 + 1 - core)
        pair_copy(o).start()
        if transposed:
            tile(i * 2 + core)
        return carry

    lax.fori_loop(0, chips, produce, 0)

    def add_pair(o):
        pair_copy(o).wait_recv()
        b = chip_at(o) * 2 + core
        at = pl.ds(pl.multiple_of(b * rows, rows), rows)
        grad[at, :] = grad[at, :] + pair_buf[o]

    def loop(lo, hi, f):
        lax.fori_loop(lo, hi, lambda j, c: (f(j), c)[1], 0)

    def send_on(o):
        add_pair(o)
        xy_copy(0, o).start()

    def z_peer(k):
        return (z + k) % rep

    def part_at(s, q):
        return pl.ds(pl.multiple_of(s * chunk_lin + q * part, part), part)

    def zr_copy(s, k, wait=False):
        if parts > 1:
            src, slot = acc.at[part_at(s, z_peer(k))], k - 1
        else:
            src, slot = acc.at[part_at(s, 0)], (z + rep - k) % rep if wait else z
        return pltpu.make_async_remote_copy(
            src, z_buf.at[s, slot], zr_s.at[s, k - 1], zr_r.at[s, k - 1], device_id={"rep": z_peer(k)},
        )

    def zg_copy(s, k, wait=False):
        at = part_at(s, (z + rep - k) % rep if wait else z)
        return pltpu.make_async_remote_copy(
            full.at[at], full.at[at], zg_s.at[s, k - 1], zg_r.at[s, k - 1], device_id={"rep": z_peer(k)},
        )

    def sum_chips(s):
        def add_chip(o, total):
            xy_copy(s, o).wait_recv()
            return total + xy_buf[s, o]

        at = pl.ds(pl.multiple_of(me * rows, rows), rows)
        total = lax.fori_loop(0, chips - 1, add_chip, grad[at, s * wide : (s + 1) * wide])
        if transposed:
            total = total.T
        for h in range(per):
            acc[pl.ds(s * chunk_lin + h, chunk_lin // per, stride=per), :] = total[:, h * LANES : (h + 1) * LANES]
        for k in range(1, rep):
            zr_copy(s, k).start()

    def sum_replicas(s):
        if parts > 1:
            own = acc[part_at(s, z), :]
            for k in range(1, rep):
                zr_copy(s, k, True).wait_recv()
                own = own + z_buf[s, k - 1]
            full[part_at(s, z), :] = own
            for k in range(1, rep):
                zg_copy(s, k).start()
        else:
            z_buf[s, z] = acc[part_at(s, 0), :]
            for k in range(1, rep):
                zr_copy(s, k, True).wait_recv()
            own = z_buf[s, 0]
            for k in range(1, rep):
                own = own + z_buf[s, k]
            full[part_at(s, 0), :] = own

    def part_of(s, k):
        return part_at(s, (z + parts - k) % parts if parts > 1 else 0)

    def rows_of(owner, s, k):
        q = (z + parts - k) % parts if parts > 1 else 0
        return pl.ds(pl.multiple_of(owner * lin + s * chunk_lin + q * part, part), part)

    def place(owner, s, k):
        return ow.at[rows_of(owner, s, k), :]

    def ag_copy(s, k, j, wait=False):
        if wait:
            src = dst = place((g + chips - j) % chips * 2 + core, s, k)
        else:
            src = dst = place(me, s, k)
        return pltpu.make_async_remote_copy(
            src, dst, ag_s.at[s, k, j], ag_r.at[s, k, j], device_id={"dp": (g + j) % chips * 2 + core},
        )

    def to_copy(s, k, j):
        at = place((g + chips - j) % chips * 2 + core, s, k)
        return pltpu.make_async_remote_copy(
            at, at, to_s.at[s, k, j], to_r.at[s, k, j], device_id={"dp": partner},
        )

    def to_wait(s, k, j):
        at = place((g + chips - j) % chips * 2 + 1 - core, s, k)
        return pltpu.make_async_remote_copy(
            at, at, to_s.at[s, k, j], to_r.at[s, k, j], device_id={"dp": partner},
        )

    def update(s, k):
        if k > 0:
            zg_copy(s, k, True).wait_recv()
        at = part_of(s, k)
        new_master, new_first, new_second = adam(full[at, :], ma[at, :], m1[at, :], m2[at, :])
        ow[rows_of(me, s, k), :] = new_master.astype(jnp.bfloat16)
        loop(1, chips, lambda j: ag_copy(s, k, j).start())
        to_copy(s, k, 0).start()
        oma[at, :] = new_master
        om1[at, :] = new_first
        om2[at, :] = new_second

    def hand_on(s, k):
        def one(j):
            ag_copy(s, k, j, True).wait_recv()
            to_copy(s, k, j).start()

        loop(1, chips, one)

    loop(0, chips - 1, send_on)
    add_pair(chips - 1)
    for s in range(1, chunks):
        loop(0, chips - 1, lambda o: xy_copy(s, o).start())
    for c in loads[4:]:
        c.wait()

    sum_chips(0)
    sum_replicas(0)
    update(0, 0)
    for s in range(1, chunks):
        sum_chips(s)
        for k in range(1, parts):
            update(s - 1, k)
        sum_replicas(s)
        update(s, 0)
        for k in range(parts):
            hand_on(s - 1, k)
    for k in range(1, parts):
        update(chunks - 1, k)
    for k in range(parts):
        hand_on(chunks - 1, k)

    outs = [
        pltpu.make_async_copy(src, dst, out_sem.at[i])
        for i, (src, dst) in enumerate([(oma, oma_hbm), (om1, om1_hbm), (om2, om2_hbm)])
    ]
    for c in outs:
        c.start()

    def ow_copy(s, b):
        at = pl.ds(pl.multiple_of(b * lin + s * chunk_lin, chunk_lin), chunk_lin)
        return pltpu.make_async_copy(ow.at[at, :], ow_hbm.at[at, :], ow_sem.at[s, b])

    for s in range(chunks):
        for k in range(parts):
            loop(0, chips, lambda j: to_wait(s, k, j).wait_recv())
        loop(0, dp, lambda b: ow_copy(s, b).start())

    loop(0, chips, lambda o: pair_copy(o).wait_send())
    for s in range(chunks):
        loop(0, chips - 1, lambda o: xy_copy(s, o).wait_send())
        for k in range(1, rep):
            zr_copy(s, k).wait_send()
            if parts > 1:
                zg_copy(s, k).wait_send()
        for k in range(parts):
            loop(1, chips, lambda j: ag_copy(s, k, j).wait_send())
            to_copy(s, k, 0).wait_send()
            loop(1, chips, lambda j: to_copy(s, k, j).wait_send())
        loop(0, dp, lambda b: ow_copy(s, b).wait())
    for c in outs:
        c.wait()


def results_kernel(*refs):
    n = len(refs) // 3
    ins, outs, held, (in_sem, out_sem) = refs[:n], refs[n : 2 * n], refs[2 * n : 3 * n], refs[3 * n :]
    loads, stores = [], []
    for i in range(n):
        size = ins[i].shape[0] // PIECES
        for p in range(PIECES):
            at = pl.ds(p * size, size)
            loads.append(pltpu.make_async_copy(ins[i].at[at, :], held[i].at[at, :], in_sem.at[i, p]))
            stores.append(pltpu.make_async_copy(held[i].at[at, :], outs[i].at[at, :], out_sem.at[i, p]))
    for c in loads:
        c.start()
    for load, store in zip(loads, stores):
        load.wait()
        store.start()
    for c in stores:
        c.wait()


def shards(dp, rep, clips, cotangent, alphas, weights, master, first_moment, second_moment):
    frames, ch = clips.shape[1:]
    params = weights.shape[0]
    own = master.shape[0]
    rows = own // ch
    lin = own // LANES
    chips = dp // 2
    transposed = rows == ch
    chunks = ch // LANES if transposed else 1
    parts = rep if lin // chunks % (16 * rep) == 0 else 1
    part = lin // chunks // parts
    plan = (frames, ch, dp, rep, rows, transposed, chunks, parts)
    anywhere = pl.BlockSpec(memory_space=pl.ANY)
    f32, bf16 = jnp.float32, jnp.bfloat16
    dma = pltpu.SemaphoreType.DMA
    outs = pl.pallas_call(
        functools.partial(step_kernel, plan),
        out_shape=(
            jax.ShapeDtypeStruct((params // LANES, LANES), bf16),
            jax.ShapeDtypeStruct((lin, LANES), f32),
            jax.ShapeDtypeStruct((lin, LANES), f32),
            jax.ShapeDtypeStruct((lin, LANES), f32),
        ),
        in_specs=[anywhere] * 7,
        out_specs=(anywhere,) * 4,
        scratch_shapes=[
            pltpu.VMEM((frames, ch), bf16),
            pltpu.VMEM((frames, ch), bf16),
            pltpu.VMEM(alphas.shape, f32),
            pltpu.VMEM((params // LANES, LANES), bf16),
            pltpu.VMEM((params // LANES, LANES), f32),
            pltpu.VMEM((params // ch, ch), bf16),
            pltpu.VMEM((lin, LANES), f32),
            pltpu.VMEM((lin, LANES), f32),
            pltpu.VMEM((lin, LANES), f32),
            pltpu.VMEM((ch // LANES, frames + 32, LANES), f32),
            pltpu.VMEM((frames, (TAPS + 1) * ch), bf16),
            pltpu.VMEM((2, ch, frames), bf16),
            pltpu.VMEM((params // ch, ch), f32),
            pltpu.VMEM((chips, rows, ch), f32),
            pltpu.VMEM((chunks, chips - 1, rows, ch // chunks), f32),
            pltpu.VMEM((lin, LANES), f32),
            pltpu.VMEM((chunks, rep, part, LANES), f32),
            pltpu.VMEM((lin, LANES), f32),
            pltpu.VMEM((params // LANES, LANES), bf16),
            pltpu.VMEM((lin, LANES), f32),
            pltpu.VMEM((lin, LANES), f32),
            pltpu.VMEM((lin, LANES), f32),
            dma((7,)),
            dma((3,)),
            dma((chunks, dp)),
            dma((chips,)), dma((chips,)),
            dma((chunks, chips)), dma((chunks, chips)),
            dma((chunks, rep)), dma((chunks, rep)),
            dma((chunks, rep)), dma((chunks, rep)),
            dma((chunks, parts, chips)), dma((chunks, parts, chips)),
            dma((chunks, parts, chips)), dma((chunks, parts, chips)),
        ],
        compiler_params=pltpu.CompilerParams(
            collective_id=0, has_side_effects=True, vmem_limit_bytes=64 * 1024 * 1024
        ),
        name="train_step",
    )(
        clips[0],
        cotangent[0],
        alphas,
        weights.reshape(params // LANES, LANES),
        master.reshape(lin, LANES),
        first_moment.reshape(lin, LANES),
        second_moment.reshape(lin, LANES),
    )
    outs = pl.pallas_call(
        results_kernel,
        out_shape=tuple(jax.ShapeDtypeStruct(o.shape, o.dtype) for o in outs),
        in_specs=[anywhere] * len(outs),
        out_specs=(anywhere,) * len(outs),
        scratch_shapes=[pltpu.VMEM(o.shape, o.dtype) for o in outs] + [dma((len(outs), PIECES))] * 2,
        compiler_params=pltpu.CompilerParams(vmem_limit_bytes=64 * 1024 * 1024),
        name="results",
    )(*outs)
    return tuple(o.reshape(-1) for o in outs)


def solution(mesh):
    return jax.shard_map(
        functools.partial(shards, mesh.shape["dp"], mesh.shape["rep"]),
        mesh=mesh,
        in_specs=(
            P(("dp", "rep"), None, None),
            P(("dp", "rep"), None, None),
            P(),
            P(),
            P("dp"),
            P("dp"),
            P("dp"),
        ),
        out_specs=(P(), P("dp"), P("dp"), P("dp")),
        check_vma=False,
    )
```

```python
import functools

import jax
import jax.numpy as jnp
from jax import lax
from jax.experimental import pallas as pl
from jax.experimental.pallas import tpu as pltpu
from jax.sharding import PartitionSpec as P

TAPS = 7
DILATION = 3
LANES = 128
SLICE = 32
PIECES = 2

BIAS_ONE = 0.9999734386011124
BIAS_TWO = 0.09520785288629041

PI_A = 3.140625
PI_B = 9.67502593994140625e-4
PI_C = 1.509957990978376432e-7
INV_PI = 0.3183098861837907

SIN = (-0.16666659712791443, 0.008333083242177963, -0.00019810810044873506, 2.6083068860316416e-06)
COS = (-0.5, 0.04166664183139801, -0.001388839678838849, 2.4761575332377106e-05, -2.607200428883516e-07)


def reduced(u):
    k = jnp.round(u * INV_PI)
    return ((u - k * PI_A) - k * PI_B) - k * PI_C


def sin_of(r, r2):
    return r + r * (r2 * (SIN[0] + r2 * (SIN[1] + r2 * (SIN[2] + r2 * SIN[3]))))


def cos_of(r2):
    return 1.0 + r2 * (COS[0] + r2 * (COS[1] + r2 * (COS[2] + r2 * (COS[3] + r2 * COS[4]))))


def dot(a, b, dims):
    return lax.dot_general(a, b, (dims, ((), ())), preferred_element_type=jnp.float32)


def adam(gradient, master, first_moment, second_moment):
    new_first = 0.9 * first_moment + 0.1 * gradient
    new_second = 0.999 * second_moment + 0.001 * gradient * gradient
    new_master = master - 0.001 * (new_first / BIAS_ONE) / (jnp.sqrt(new_second / BIAS_TWO) + 1e-08)
    return new_master, new_first, new_second


def step_kernel(
    plan,
    clip_hbm, cot_hbm, alpha_hbm, w_hbm, ma_hbm, m1_hbm, m2_hbm,
    ow_hbm, oma_hbm, om1_hbm, om2_hbm,
    clip, cot, alpha_ref, w_lin, w32, w_mat, ma, m1, m2,
    padded, win, hid, bak, d_hid, lhs, grad, pair_buf, xy_buf, acc, z_buf, full, ow, oma, om1, om2,
    in_sem, out_sem, ow_sem, pair_s, pair_r, xy_s, xy_r, zr_s, zr_r, zg_s, zg_r,
    ag_s, ag_r, to_s, to_r,
):
    frames, ch, dp, rep, rows, transposed, chunks, parts = plan
    chips = dp // 2
    lin = rows * ch // LANES
    chunk_lin = lin // chunks
    part = chunk_lin // parts
    wide = ch // chunks
    me = lax.axis_index("dp")
    z = lax.axis_index("rep")
    core = me % 2
    g = me // 2
    partner = g * 2 + 1 - core

    loads = [
        pltpu.make_async_copy(s, d, in_sem.at[i])
        for i, (s, d) in enumerate(
            [(alpha_hbm, alpha_ref), (clip_hbm, clip), (w_hbm, w_lin), (cot_hbm, cot), (ma_hbm, ma), (m1_hbm, m1), (m2_hbm, m2)]
        )
    ]
    for c in loads:
        c.start()

    barrier = pltpu.get_barrier_semaphore()
    pl.semaphore_signal(barrier, inc=1, device_id={"dp": partner})
    for k in range(1, chips):
        pl.semaphore_signal(barrier, inc=1, device_id={"dp": (g + k) % chips * 2 + core})
    for k in range(1, rep):
        pl.semaphore_signal(barrier, inc=1, device_id={"rep": (z + k) % rep})

    reach = DILATION * (TAPS // 2)
    base = 16
    split = TAPS * ch

    loads[0].wait()
    loads[1].wait()
    a0 = alpha_ref[0:1, :]
    inv0 = 1.0 / a0
    for h in range(ch // LANES):
        padded[h, 0:base, :] = jnp.zeros((base, LANES), jnp.float32)
        padded[h, base + frames : base + frames + base, :] = jnp.zeros((base, LANES), jnp.float32)

    def activate(c, carry):
        for i in range(2):
            at = pl.multiple_of((2 * c + i) * SLICE, SLICE)
            v = clip[pl.ds(at, SLICE), :].astype(jnp.float32)
            r = reduced(a0 * v)
            s = sin_of(r, r * r)
            first = v + s * s * inv0
            for h in range(ch // LANES):
                padded[h, pl.ds(base + at, SLICE), :] = first[:, h * LANES : (h + 1) * LANES]
        return carry

    lax.fori_loop(0, frames // (2 * SLICE), activate, 0)
    for k in range(TAPS):
        for h in range(ch // LANES):
            start = base + DILATION * k - reach
            win[:, k * ch + h * LANES : k * ch + (h + 1) * LANES] = padded[
                h, start : start + frames, :
            ].astype(jnp.bfloat16)

    loads[2].wait()
    per = ch // LANES
    piece = 256

    def relay(c, carry):
        at = pl.ds(pl.multiple_of(c * piece * per, piece * per), piece * per)
        w32[at, :] = w_lin[at, :].astype(jnp.float32)
        to = pl.ds(pl.multiple_of(c * piece, piece), piece)
        for h in range(per):
            w_mat[to, h * LANES : (h + 1) * LANES] = w32[
                pl.ds(c * piece * per + h, piece, stride=per), :
            ].astype(jnp.bfloat16)
        return carry

    lax.fori_loop(0, (split + ch) // piece, relay, 0)

    loads[3].wait()
    lhs[1] = cot[...].T

    a1 = alpha_ref[1:2, :]
    inv1 = 1.0 / a1
    chunk = 256

    for c in range(frames // chunk):
        at = slice(c * chunk, (c + 1) * chunk)
        hid[at, :] = dot(win[at, :split], w_mat[:split, :], ((1,), (0,)))
        bak[at, :] = dot(cot[at, :], w_mat[split:, :], ((1,), (1,)))
    for c in range(frames // chunk):
        at = slice(c * chunk, (c + 1) * chunk)
        for i in range(c * chunk, (c + 1) * chunk, SLICE):
            hidden = hid[i : i + SLICE, :]
            r = reduced(a1 * hidden)
            r2 = r * r
            s = sin_of(r, r2)
            win[i : i + SLICE, split : split + ch] = (hidden + s * s * inv1).astype(jnp.bfloat16)
            d_hid[i : i + SLICE, :] = (bak[i : i + SLICE, :] * (1.0 + 2.0 * s * cos_of(r2))).astype(jnp.bfloat16)
        lhs[0, :, at] = d_hid[at, :].T

    def block(b):
        return grad.at[pl.ds(pl.multiple_of(b * rows, rows), rows), :]

    def tile(t):
        side = t // TAPS
        part_of = win[:, pl.ds(pl.multiple_of(t * ch, ch), ch)]
        if transposed:
            value = dot(lhs[side], part_of, ((1,), (0,)))
        else:
            value = dot(lhs[side], part_of, ((1,), (0,))).T
        grad[pl.ds(pl.multiple_of(t * ch, ch), ch), :] = value

    if not transposed:
        lax.fori_loop(0, TAPS, lambda t, c: (tile(t), c)[1], 0)
        second = dot(lhs[1], win[:, split : split + ch], ((1,), (0,)))
        grad[split : split + ch, :] = second.T

    pl.semaphore_wait(barrier, chips + rep - 1)

    def chip_at(o):
        return (g + 1 + o) % chips

    def pair_copy(o):
        return pltpu.make_async_remote_copy(
            block(chip_at(o) * 2 + 1 - core), pair_buf.at[o], pair_s.at[o], pair_r.at[o],
            device_id={"dp": partner},
        )

    def xy_copy(s, o):
        to = chip_at(o)
        return pltpu.make_async_remote_copy(
            block(to * 2 + core).at[:, s * wide : (s + 1) * wide], xy_buf.at[s, o], xy_s.at[s, o], xy_r.at[s, o],
            device_id={"dp": to * 2 + core},
        )

    def add_pair(o):
        pair_copy(o).wait_recv()
        b = chip_at(o) * 2 + core
        at = pl.ds(pl.multiple_of(b * rows, rows), rows)
        grad[at, :] = grad[at, :] + pair_buf[o]

    def loop(lo, hi, f):
        lax.fori_loop(lo, hi, lambda j, c: (f(j), c)[1], 0)

    def send_on(o):
        add_pair(o)
        xy_copy(0, o).start()

    def z_peer(k):
        return (z + k) % rep

    def part_at(s, q):
        return pl.ds(pl.multiple_of(s * chunk_lin + q * part, part), part)

    def zr_copy(s, k, wait=False):
        if parts > 1:
            src, slot = acc.at[part_at(s, z_peer(k))], k - 1
        else:
            src, slot = acc.at[part_at(s, 0)], (z + rep - k) % rep if wait else z
        return pltpu.make_async_remote_copy(
            src, z_buf.at[s, slot], zr_s.at[s, k - 1], zr_r.at[s, k - 1], device_id={"rep": z_peer(k)},
        )

    def zg_copy(s, k, wait=False):
        at = part_at(s, (z + rep - k) % rep if wait else z)
        return pltpu.make_async_remote_copy(
            full.at[at], full.at[at], zg_s.at[s, k - 1], zg_r.at[s, k - 1], device_id={"rep": z_peer(k)},
        )

    def sum_chips(s):
        def add_chip(o, total):
            xy_copy(s, o).wait_recv()
            return total + xy_buf[s, o]

        at = pl.ds(pl.multiple_of(me * rows, rows), rows)
        total = lax.fori_loop(0, chips - 1, add_chip, grad[at, s * wide : (s + 1) * wide])
        if transposed:
            total = total.T
        for h in range(per):
            acc[pl.ds(s * chunk_lin + h, chunk_lin // per, stride=per), :] = total[:, h * LANES : (h + 1) * LANES]
        for k in range(1, rep):
            zr_copy(s, k).start()

    def sum_replicas(s):
        if parts > 1:
            own = acc[part_at(s, z), :]
            for k in range(1, rep):
                zr_copy(s, k, True).wait_recv()
                own = own + z_buf[s, k - 1]
            full[part_at(s, z), :] = own
            for k in range(1, rep):
                zg_copy(s, k).start()
        else:
            z_buf[s, z] = acc[part_at(s, 0), :]
            for k in range(1, rep):
                zr_copy(s, k, True).wait_recv()
            own = z_buf[s, 0]
            for k in range(1, rep):
                own = own + z_buf[s, k]
            full[part_at(s, 0), :] = own

    def part_of(s, k):
        return part_at(s, (z + parts - k) % parts if parts > 1 else 0)

    def rows_of(owner, s, k):
        q = (z + parts - k) % parts if parts > 1 else 0
        return pl.ds(pl.multiple_of(owner * lin + s * chunk_lin + q * part, part), part)

    def place(owner, s, k):
        return ow.at[rows_of(owner, s, k), :]

    def ag_copy(s, k, j, wait=False):
        if wait:
            src = dst = place((g + chips - j) % chips * 2 + core, s, k)
        else:
            src = dst = place(me, s, k)
        return pltpu.make_async_remote_copy(
            src, dst, ag_s.at[s, k, j], ag_r.at[s, k, j], device_id={"dp": (g + j) % chips * 2 + core},
        )

    def to_copy(s, k, j):
        at = place((g + chips - j) % chips * 2 + core, s, k)
        return pltpu.make_async_remote_copy(
            at, at, to_s.at[s, k, j], to_r.at[s, k, j], device_id={"dp": partner},
        )

    def to_wait(s, k, j):
        at = place((g + chips - j) % chips * 2 + 1 - core, s, k)
        return pltpu.make_async_remote_copy(
            at, at, to_s.at[s, k, j], to_r.at[s, k, j], device_id={"dp": partner},
        )

    def update(s, k):
        if k > 0:
            zg_copy(s, k, True).wait_recv()
        at = part_of(s, k)
        new_master, new_first, new_second = adam(full[at, :], ma[at, :], m1[at, :], m2[at, :])
        ow[rows_of(me, s, k), :] = new_master.astype(jnp.bfloat16)
        loop(1, chips, lambda j: ag_copy(s, k, j).start())
        to_copy(s, k, 0).start()
        oma[at, :] = new_master
        om1[at, :] = new_first
        om2[at, :] = new_second

    def hand_on(s, k):
        def one(j):
            ag_copy(s, k, j, True).wait_recv()
            to_copy(s, k, j).start()

        loop(1, chips, one)

    def produce(o):
        i = chip_at(o)
        if transposed:
            tile(i * 2 + 1 - core)
        pair_copy(o).start()
        if transposed:
            tile(i * 2 + core)

    def produce_and_send(o):
        produce(o)
        send_on(o - 1)

    produce(0)
    loop(1, chips, produce_and_send)
    add_pair(chips - 1)
    for s in range(1, chunks):

        def follow(o):
            xy_copy(s - 1, o).wait_send()
            xy_copy(s, o).start()

        loop(0, chips - 1, follow)
    for c in loads[4:]:
        c.wait()

    sum_chips(0)
    sum_replicas(0)
    update(0, 0)
    for s in range(1, chunks):
        sum_chips(s)
        for k in range(1, parts):
            update(s - 1, k)
        sum_replicas(s)
        update(s, 0)
        for k in range(parts):
            hand_on(s - 1, k)
    for k in range(1, parts):
        update(chunks - 1, k)
    for k in range(parts):
        hand_on(chunks - 1, k)

    outs = [
        pltpu.make_async_copy(src, dst, out_sem.at[i])
        for i, (src, dst) in enumerate([(oma, oma_hbm), (om1, om1_hbm), (om2, om2_hbm)])
    ]
    for c in outs:
        c.start()

    def ow_copy(s, b):
        at = pl.ds(pl.multiple_of(b * lin + s * chunk_lin, chunk_lin), chunk_lin)
        return pltpu.make_async_copy(ow.at[at, :], ow_hbm.at[at, :], ow_sem.at[s, b])

    for s in range(chunks):
        for k in range(parts):
            loop(0, chips, lambda j: to_wait(s, k, j).wait_recv())
        loop(0, dp, lambda b: ow_copy(s, b).start())

    loop(0, chips, lambda o: pair_copy(o).wait_send())
    for s in range(chunks):
        if s == chunks - 1:
            loop(0, chips - 1, lambda o: xy_copy(s, o).wait_send())
        for k in range(1, rep):
            zr_copy(s, k).wait_send()
            if parts > 1:
                zg_copy(s, k).wait_send()
        for k in range(parts):
            loop(1, chips, lambda j: ag_copy(s, k, j).wait_send())
            to_copy(s, k, 0).wait_send()
            loop(1, chips, lambda j: to_copy(s, k, j).wait_send())
        loop(0, dp, lambda b: ow_copy(s, b).wait())
    for c in outs:
        c.wait()


def results_kernel(*refs):
    n = len(refs) // 3
    ins, outs, held, (in_sem, out_sem) = refs[:n], refs[n : 2 * n], refs[2 * n : 3 * n], refs[3 * n :]
    loads, stores = [], []
    for i in range(n):
        size = ins[i].shape[0] // PIECES
        for p in range(PIECES):
            at = pl.ds(p * size, size)
            loads.append(pltpu.make_async_copy(ins[i].at[at, :], held[i].at[at, :], in_sem.at[i, p]))
            stores.append(pltpu.make_async_copy(held[i].at[at, :], outs[i].at[at, :], out_sem.at[i, p]))
    for c in loads:
        c.start()
    for load, store in zip(loads, stores):
        load.wait()
        store.start()
    for c in stores:
        c.wait()


def shards(dp, rep, clips, cotangent, alphas, weights, master, first_moment, second_moment):
    frames, ch = clips.shape[1:]
    params = weights.shape[0]
    own = master.shape[0]
    rows = own // ch
    lin = own // LANES
    chips = dp // 2
    transposed = rows == ch
    chunks = ch // LANES if transposed else 1
    parts = rep if lin // chunks % (16 * rep) == 0 else 1
    part = lin // chunks // parts
    plan = (frames, ch, dp, rep, rows, transposed, chunks, parts)
    anywhere = pl.BlockSpec(memory_space=pl.ANY)
    f32, bf16 = jnp.float32, jnp.bfloat16
    dma = pltpu.SemaphoreType.DMA
    outs = pl.pallas_call(
        functools.partial(step_kernel, plan),
        out_shape=(
            jax.ShapeDtypeStruct((params // LANES, LANES), bf16),
            jax.ShapeDtypeStruct((lin, LANES), f32),
            jax.ShapeDtypeStruct((lin, LANES), f32),
            jax.ShapeDtypeStruct((lin, LANES), f32),
        ),
        in_specs=[anywhere] * 7,
        out_specs=(anywhere,) * 4,
        scratch_shapes=[
            pltpu.VMEM((frames, ch), bf16),
            pltpu.VMEM((frames, ch), bf16),
            pltpu.VMEM(alphas.shape, f32),
            pltpu.VMEM((params // LANES, LANES), bf16),
            pltpu.VMEM((params // LANES, LANES), f32),
            pltpu.VMEM((params // ch, ch), bf16),
            pltpu.VMEM((lin, LANES), f32),
            pltpu.VMEM((lin, LANES), f32),
            pltpu.VMEM((lin, LANES), f32),
            pltpu.VMEM((ch // LANES, frames + 32, LANES), f32),
            pltpu.VMEM((frames, (TAPS + 1) * ch), bf16),
            pltpu.VMEM((frames, ch), f32),
            pltpu.VMEM((frames, ch), f32),
            pltpu.VMEM((frames, ch), bf16),
            pltpu.VMEM((2, ch, frames), bf16),
            pltpu.VMEM((params // ch, ch), f32),
            pltpu.VMEM((chips, rows, ch), f32),
            pltpu.VMEM((chunks, chips - 1, rows, ch // chunks), f32),
            pltpu.VMEM((lin, LANES), f32),
            pltpu.VMEM((chunks, rep, part, LANES), f32),
            pltpu.VMEM((lin, LANES), f32),
            pltpu.VMEM((params // LANES, LANES), bf16),
            pltpu.VMEM((lin, LANES), f32),
            pltpu.VMEM((lin, LANES), f32),
            pltpu.VMEM((lin, LANES), f32),
            dma((7,)),
            dma((3,)),
            dma((chunks, dp)),
            dma((chips,)), dma((chips,)),
            dma((chunks, chips)), dma((chunks, chips)),
            dma((chunks, rep)), dma((chunks, rep)),
            dma((chunks, rep)), dma((chunks, rep)),
            dma((chunks, parts, chips)), dma((chunks, parts, chips)),
            dma((chunks, parts, chips)), dma((chunks, parts, chips)),
        ],
        compiler_params=pltpu.CompilerParams(
            collective_id=0, has_side_effects=True, vmem_limit_bytes=64 * 1024 * 1024
        ),
        name="train_step",
    )(
        clips[0],
        cotangent[0],
        alphas,
        weights.reshape(params // LANES, LANES),
        master.reshape(lin, LANES),
        first_moment.reshape(lin, LANES),
        second_moment.reshape(lin, LANES),
    )
    outs = pl.pallas_call(
        results_kernel,
        out_shape=tuple(jax.ShapeDtypeStruct(o.shape, o.dtype) for o in outs),
        in_specs=[anywhere] * len(outs),
        out_specs=(anywhere,) * len(outs),
        scratch_shapes=[pltpu.VMEM(o.shape, o.dtype) for o in outs] + [dma((len(outs), PIECES))] * 2,
        compiler_params=pltpu.CompilerParams(vmem_limit_bytes=64 * 1024 * 1024),
        name="results",
    )(*outs)
    return tuple(o.reshape(-1) for o in outs)


def solution(mesh):
    return jax.shard_map(
        functools.partial(shards, mesh.shape["dp"], mesh.shape["rep"]),
        mesh=mesh,
        in_specs=(
            P(("dp", "rep"), None, None),
            P(("dp", "rep"), None, None),
            P(),
            P(),
            P("dp"),
            P("dp"),
            P("dp"),
        ),
        out_specs=(P(), P("dp"), P("dp"), P("dp")),
        check_vma=False,
    )
```

```python
import functools

import jax
import jax.numpy as jnp
from jax import lax
from jax.experimental import pallas as pl
from jax.experimental.pallas import tpu as pltpu
from jax.sharding import PartitionSpec as P

TAPS = 7
DILATION = 3
LANES = 128
SLICE = 32
PIECES = 4
CHUNKS = 4

BIAS_ONE = 0.9999734386011124
BIAS_TWO = 0.09520785288629041

PI_A = 3.140625
PI_B = 9.67502593994140625e-4
PI_C = 1.509957990978376432e-7
INV_PI = 0.3183098861837907

SIN = (-0.16666659712791443, 0.008333083242177963, -0.00019810810044873506, 2.6083068860316416e-06)
COS = (-0.5, 0.04166664183139801, -0.001388839678838849, 2.4761575332377106e-05, -2.607200428883516e-07)


def reduced(u):
    k = jnp.round(u * INV_PI)
    return ((u - k * PI_A) - k * PI_B) - k * PI_C


def sin_of(r, r2):
    return r + r * (r2 * (SIN[0] + r2 * (SIN[1] + r2 * (SIN[2] + r2 * SIN[3]))))


def cos_of(r2):
    return 1.0 + r2 * (COS[0] + r2 * (COS[1] + r2 * (COS[2] + r2 * (COS[3] + r2 * COS[4]))))


def dot(a, b, dims):
    return lax.dot_general(a, b, (dims, ((), ())), preferred_element_type=jnp.float32)


def adam(gradient, master, first_moment, second_moment):
    new_first = 0.9 * first_moment + 0.1 * gradient
    new_second = 0.999 * second_moment + 0.001 * gradient * gradient
    new_master = master - 0.001 * (new_first / BIAS_ONE) / (jnp.sqrt(new_second / BIAS_TWO) + 1e-08)
    return new_master, new_first, new_second


def step_kernel(
    plan,
    clip_hbm, cot_hbm, alpha_hbm, w_hbm, ma_hbm, m1_hbm, m2_hbm,
    ow_hbm, oma_hbm, om1_hbm, om2_hbm,
    clip, cot, alpha_ref, w_lin, w32, w_mat, ma, m1, m2,
    padded, win, hid, bak, d_hid, lhs, grad, pair_buf, xy_buf, acc, z_buf, full, ow, oma, om1, om2,
    in_sem, out_sem, ow_sem, pair_s, pair_r, xy_s, xy_r, zr_s, zr_r, zg_s, zg_r,
    ag_s, ag_r, to_s, to_r,
):
    frames, ch, dp, rep, rows, whole, chunks, parts = plan
    chips = dp // 2
    lin = rows * ch // LANES
    chunk_lin = lin // chunks
    part = chunk_lin // parts
    tall = rows // chunks
    me = lax.axis_index("dp")
    z = lax.axis_index("rep")
    core = me % 2
    g = me // 2
    partner = g * 2 + 1 - core

    loads = [
        pltpu.make_async_copy(s, d, in_sem.at[i])
        for i, (s, d) in enumerate(
            [(alpha_hbm, alpha_ref), (clip_hbm, clip), (w_hbm, w_lin), (cot_hbm, cot), (ma_hbm, ma), (m1_hbm, m1), (m2_hbm, m2)]
        )
    ]
    for c in loads:
        c.start()

    barrier = pltpu.get_barrier_semaphore()
    pl.semaphore_signal(barrier, inc=1, device_id={"dp": partner})
    for k in range(1, chips):
        pl.semaphore_signal(barrier, inc=1, device_id={"dp": (g + k) % chips * 2 + core})
    for k in range(1, rep):
        pl.semaphore_signal(barrier, inc=1, device_id={"rep": (z + k) % rep})

    reach = DILATION * (TAPS // 2)
    base = 16
    split = TAPS * ch

    loads[0].wait()
    loads[1].wait()
    a0 = alpha_ref[0:1, :]
    inv0 = 1.0 / a0
    for h in range(ch // LANES):
        padded[h, 0:base, :] = jnp.zeros((base, LANES), jnp.float32)
        padded[h, base + frames : base + frames + base, :] = jnp.zeros((base, LANES), jnp.float32)

    def activate(c, carry):
        for i in range(2):
            at = pl.multiple_of((2 * c + i) * SLICE, SLICE)
            v = clip[pl.ds(at, SLICE), :].astype(jnp.float32)
            r = reduced(a0 * v)
            s = sin_of(r, r * r)
            first = v + s * s * inv0
            for h in range(ch // LANES):
                padded[h, pl.ds(base + at, SLICE), :] = first[:, h * LANES : (h + 1) * LANES]
        return carry

    lax.fori_loop(0, frames // (2 * SLICE), activate, 0)
    for k in range(TAPS):
        for h in range(ch // LANES):
            start = base + DILATION * k - reach
            win[:, k * ch + h * LANES : k * ch + (h + 1) * LANES] = padded[
                h, start : start + frames, :
            ].astype(jnp.bfloat16)

    loads[2].wait()
    per = ch // LANES
    piece = 256

    def relay(c, carry):
        at = pl.ds(pl.multiple_of(c * piece * per, piece * per), piece * per)
        w32[at, :] = w_lin[at, :].astype(jnp.float32)
        to = pl.ds(pl.multiple_of(c * piece, piece), piece)
        for h in range(per):
            w_mat[to, h * LANES : (h + 1) * LANES] = w32[
                pl.ds(c * piece * per + h, piece, stride=per), :
            ].astype(jnp.bfloat16)
        return carry

    lax.fori_loop(0, (split + ch) // piece, relay, 0)

    loads[3].wait()
    lhs[1] = cot[...].T

    a1 = alpha_ref[1:2, :]
    inv1 = 1.0 / a1
    chunk = 256

    def multiply(c):
        at = slice(c * chunk, (c + 1) * chunk)
        hid[at, :] = dot(win[at, :split], w_mat[:split, :], ((1,), (0,)))
        bak[at, :] = dot(cot[at, :], w_mat[split:, :], ((1,), (1,)))

    multiply(0)
    for c in range(frames // chunk):
        at = slice(c * chunk, (c + 1) * chunk)
        if (c + 1) * chunk < frames:
            multiply(c + 1)
        for i in range(c * chunk, (c + 1) * chunk, SLICE):
            hidden = hid[i : i + SLICE, :]
            r = reduced(a1 * hidden)
            r2 = r * r
            s = sin_of(r, r2)
            win[i : i + SLICE, split : split + ch] = (hidden + s * s * inv1).astype(jnp.bfloat16)
            d_hid[i : i + SLICE, :] = (bak[i : i + SLICE, :] * (1.0 + 2.0 * s * cos_of(r2))).astype(jnp.bfloat16)
        lhs[0, :, at] = d_hid[at, :].T

    def block(b):
        return grad.at[pl.ds(pl.multiple_of(b * rows, rows), rows), :]

    def chunk_rows(b, s):
        return pl.ds(pl.multiple_of(b * rows + s * tall, tall), tall)

    def chunk_of(b, s):
        return grad.at[chunk_rows(b, s), :]

    def tile(t):
        part_of = win[:, pl.ds(pl.multiple_of(t * ch, ch), ch)]
        value = dot(lhs[t // TAPS], part_of, ((1,), (0,)))
        grad[pl.ds(pl.multiple_of(t * ch, ch), ch), :] = value.T

    if not whole:
        lax.fori_loop(0, TAPS + 1, lambda t, c: (tile(t), c)[1], 0)

    pl.semaphore_wait(barrier, chips + rep - 1)

    def chip_at(o):
        return (g + 1 + o) % chips

    def pair_copy(o):
        return pltpu.make_async_remote_copy(
            block(chip_at(o) * 2 + 1 - core), pair_buf.at[o], pair_s.at[o], pair_r.at[o],
            device_id={"dp": partner},
        )

    def xy_copy(s, o):
        to = chip_at(o)
        return pltpu.make_async_remote_copy(
            chunk_of(to * 2 + core, s), xy_buf.at[s, o], xy_s.at[s, o], xy_r.at[s, o],
            device_id={"dp": to * 2 + core},
        )

    def add_pair(o):
        pair_copy(o).wait_recv()
        b = chip_at(o) * 2 + core
        at = pl.ds(pl.multiple_of(b * rows, rows), rows)
        grad[at, :] = grad[at, :] + pair_buf[o]

    def loop(lo, hi, f):
        lax.fori_loop(lo, hi, lambda j, c: (f(j), c)[1], 0)

    def send_on(o):
        add_pair(o)
        xy_copy(0, o).start()

    def z_peer(k):
        return (z + k) % rep

    def part_at(s, q):
        return pl.ds(pl.multiple_of(s * chunk_lin + q * part, part), part)

    def zr_copy(s, k, wait=False):
        if parts > 1:
            src, slot = acc.at[part_at(s, z_peer(k))], k - 1
        else:
            src, slot = acc.at[part_at(s, 0)], (z + rep - k) % rep if wait else z
        return pltpu.make_async_remote_copy(
            src, z_buf.at[s, slot], zr_s.at[s, k - 1], zr_r.at[s, k - 1], device_id={"rep": z_peer(k)},
        )

    def zg_copy(s, k, wait=False):
        at = part_at(s, (z + rep - k) % rep if wait else z)
        return pltpu.make_async_remote_copy(
            full.at[at], full.at[at], zg_s.at[s, k - 1], zg_r.at[s, k - 1], device_id={"rep": z_peer(k)},
        )

    def sum_chips(s):
        def add_chip(o, total):
            xy_copy(s, o).wait_recv()
            return total + xy_buf[s, o]

        total = lax.fori_loop(0, chips - 1, add_chip, grad[chunk_rows(me, s), :])
        for h in range(per):
            acc[pl.ds(s * chunk_lin + h, chunk_lin // per, stride=per), :] = total[:, h * LANES : (h + 1) * LANES]
        for k in range(1, rep):
            zr_copy(s, k).start()

    def sum_replicas(s):
        if parts > 1:
            own = acc[part_at(s, z), :]
            for k in range(1, rep):
                zr_copy(s, k, True).wait_recv()
                own = own + z_buf[s, k - 1]
            full[part_at(s, z), :] = own
            for k in range(1, rep):
                zg_copy(s, k).start()
        else:
            z_buf[s, z] = acc[part_at(s, 0), :]
            for k in range(1, rep):
                zr_copy(s, k, True).wait_recv()
            own = z_buf[s, 0]
            for k in range(1, rep):
                own = own + z_buf[s, k]
            full[part_at(s, 0), :] = own

    def lin_at(s, owner=0):
        return pl.ds(pl.multiple_of(owner * lin + s * chunk_lin, chunk_lin), chunk_lin)

    def place(owner, s):
        return ow.at[lin_at(s, owner), :]

    def ag_copy(s, j, wait=False):
        at = place((g + chips - j) % chips * 2 + core if wait else me, s)
        return pltpu.make_async_remote_copy(
            at, at, ag_s.at[s, j], ag_r.at[s, j], device_id={"dp": (g + j) % chips * 2 + core},
        )

    def to_copy(s, j, wait=False):
        at = place((g + chips - j) % chips * 2 + (1 - core if wait else core), s)
        return pltpu.make_async_remote_copy(
            at, at, to_s.at[s, j], to_r.at[s, j], device_id={"dp": partner},
        )

    def ow_copy(s, b):
        at = lin_at(s, b)
        return pltpu.make_async_copy(ow.at[at, :], ow_hbm.at[at, :], ow_sem.at[s, b])

    def outs(s):
        at = lin_at(s)
        return [
            pltpu.make_async_copy(src.at[at, :], dst.at[at, :], out_sem.at[s, i])
            for i, (src, dst) in enumerate([(oma, oma_hbm), (om1, om1_hbm), (om2, om2_hbm)])
        ]

    def update(s):
        if parts > 1:
            for k in range(1, rep):
                zg_copy(s, k, True).wait_recv()
        at = lin_at(s)
        new_master, new_first, new_second = adam(full[at, :], ma[at, :], m1[at, :], m2[at, :])
        ow[lin_at(s, me), :] = new_master.astype(jnp.bfloat16)
        loop(1, chips, lambda j: ag_copy(s, j).start())
        to_copy(s, 0).start()
        oma[at, :] = new_master
        om1[at, :] = new_first
        om2[at, :] = new_second
        for c in outs(s):
            c.start()

    def hand_on(s):
        def one(j):
            ag_copy(s, j, True).wait_recv()
            to_copy(s, j).start()

        loop(1, chips, one)

    def store(s):
        loop(0, chips, lambda j: to_copy(s, j, True).wait_recv())
        loop(0, dp, lambda b: ow_copy(s, b).start())

    def follow(s):
        def one(o):
            xy_copy(s - 1, o).wait_send()
            xy_copy(s, o).start()

        loop(0, chips - 1, one)

    def produce(o):
        i = chip_at(o)
        if whole:
            tile(i * 2 + 1 - core)
        pair_copy(o).start()
        if whole:
            tile(i * 2 + core)

    def produce_and_send(o):
        produce(o)
        send_on(o - 1)

    produce(0)
    loop(1, chips, produce_and_send)
    add_pair(chips - 1)
    for c in loads[4:]:
        c.wait()
    for t in range(chunks + 4):
        if 0 < t + 1 < chunks:
            follow(t + 1)
        for late, stage in enumerate((sum_chips, sum_replicas, update, hand_on, store)):
            if 0 <= t - late < chunks:
                stage(t - late)

    loop(0, chips, lambda o: pair_copy(o).wait_send())
    loop(0, chips - 1, lambda o: xy_copy(chunks - 1, o).wait_send())
    for s in range(chunks):
        for k in range(1, rep):
            zr_copy(s, k).wait_send()
            if parts > 1:
                zg_copy(s, k).wait_send()
        loop(1, chips, lambda j: ag_copy(s, j).wait_send())
        loop(0, chips, lambda j: to_copy(s, j).wait_send())
        loop(0, dp, lambda b: ow_copy(s, b).wait())
        for c in outs(s):
            c.wait()


def results_kernel(*refs):
    n = len(refs) // 3
    ins, outs, held, (in_sem, out_sem) = refs[:n], refs[n : 2 * n], refs[2 * n : 3 * n], refs[3 * n :]
    loads, stores = [], []
    for i in range(n):
        size = ins[i].shape[0] // PIECES
        for p in range(PIECES):
            at = pl.ds(p * size, size)
            loads.append(pltpu.make_async_copy(ins[i].at[at, :], held[i].at[at, :], in_sem.at[i, p]))
            stores.append(pltpu.make_async_copy(held[i].at[at, :], outs[i].at[at, :], out_sem.at[i, p]))
    for c in loads:
        c.start()
    for load, store in zip(loads, stores):
        load.wait()
        store.start()
    for c in stores:
        c.wait()


def shards(dp, rep, clips, cotangent, alphas, weights, master, first_moment, second_moment):
    frames, ch = clips.shape[1:]
    params = weights.shape[0]
    own = master.shape[0]
    rows = own // ch
    lin = own // LANES
    chips = dp // 2
    whole = rows == ch
    chunks = CHUNKS if whole else 1
    parts = rep if lin // chunks % (16 * rep) == 0 else 1
    part = lin // chunks // parts
    plan = (frames, ch, dp, rep, rows, whole, chunks, parts)
    anywhere = pl.BlockSpec(memory_space=pl.ANY)
    f32, bf16 = jnp.float32, jnp.bfloat16
    dma = pltpu.SemaphoreType.DMA
    outs = pl.pallas_call(
        functools.partial(step_kernel, plan),
        out_shape=(
            jax.ShapeDtypeStruct((params // LANES, LANES), bf16),
            jax.ShapeDtypeStruct((lin, LANES), f32),
            jax.ShapeDtypeStruct((lin, LANES), f32),
            jax.ShapeDtypeStruct((lin, LANES), f32),
        ),
        in_specs=[anywhere] * 7,
        out_specs=(anywhere,) * 4,
        scratch_shapes=[
            pltpu.VMEM((frames, ch), bf16),
            pltpu.VMEM((frames, ch), bf16),
            pltpu.VMEM(alphas.shape, f32),
            pltpu.VMEM((params // LANES, LANES), bf16),
            pltpu.VMEM((params // LANES, LANES), f32),
            pltpu.VMEM((params // ch, ch), bf16),
            pltpu.VMEM((lin, LANES), f32),
            pltpu.VMEM((lin, LANES), f32),
            pltpu.VMEM((lin, LANES), f32),
            pltpu.VMEM((ch // LANES, frames + 32, LANES), f32),
            pltpu.VMEM((frames, (TAPS + 1) * ch), bf16),
            pltpu.VMEM((frames, ch), f32),
            pltpu.VMEM((frames, ch), f32),
            pltpu.VMEM((frames, ch), bf16),
            pltpu.VMEM((2, ch, frames), bf16),
            pltpu.VMEM((params // ch, ch), f32),
            pltpu.VMEM((chips, rows, ch), f32),
            pltpu.VMEM((chunks, chips - 1, rows // chunks, ch), f32),
            pltpu.VMEM((lin, LANES), f32),
            pltpu.VMEM((chunks, rep, part, LANES), f32),
            pltpu.VMEM((lin, LANES), f32),
            pltpu.VMEM((params // LANES, LANES), bf16),
            pltpu.VMEM((lin, LANES), f32),
            pltpu.VMEM((lin, LANES), f32),
            pltpu.VMEM((lin, LANES), f32),
            dma((7,)),
            dma((chunks, 3)),
            dma((chunks, dp)),
            dma((chips,)), dma((chips,)),
            dma((chunks, chips)), dma((chunks, chips)),
            dma((chunks, rep)), dma((chunks, rep)),
            dma((chunks, rep)), dma((chunks, rep)),
            dma((chunks, chips)), dma((chunks, chips)),
            dma((chunks, chips)), dma((chunks, chips)),
        ],
        compiler_params=pltpu.CompilerParams(
            collective_id=0, has_side_effects=True, vmem_limit_bytes=64 * 1024 * 1024
        ),
        name="train_step",
    )(
        clips[0],
        cotangent[0],
        alphas,
        weights.reshape(params // LANES, LANES),
        master.reshape(lin, LANES),
        first_moment.reshape(lin, LANES),
        second_moment.reshape(lin, LANES),
    )
    outs = pl.pallas_call(
        results_kernel,
        out_shape=tuple(jax.ShapeDtypeStruct(o.shape, o.dtype) for o in outs),
        in_specs=[anywhere] * len(outs),
        out_specs=(anywhere,) * len(outs),
        scratch_shapes=[pltpu.VMEM(o.shape, o.dtype) for o in outs] + [dma((len(outs), PIECES))] * 2,
        compiler_params=pltpu.CompilerParams(vmem_limit_bytes=64 * 1024 * 1024),
        name="results",
    )(*outs)
    return tuple(o.reshape(-1) for o in outs)


def solution(mesh):
    return jax.shard_map(
        functools.partial(shards, mesh.shape["dp"], mesh.shape["rep"]),
        mesh=mesh,
        in_specs=(
            P(("dp", "rep"), None, None),
            P(("dp", "rep"), None, None),
            P(),
            P(),
            P("dp"),
            P("dp"),
            P("dp"),
        ),
        out_specs=(P(), P("dp"), P("dp"), P("dp")),
        check_vma=False,
    )
```

```python
import functools

import jax
import jax.numpy as jnp
from jax import lax
from jax.experimental import pallas as pl
from jax.experimental.pallas import tpu as pltpu
from jax.sharding import PartitionSpec as P

TAPS = 7
DILATION = 3
LANES = 128
SLICE = 32
PIECES = 4
CHUNKS = 4

BIAS_ONE = 0.9999734386011124
BIAS_TWO = 0.09520785288629041

PI_A = 3.140625
PI_B = 9.67502593994140625e-4
PI_C = 1.509957990978376432e-7
INV_PI = 0.3183098861837907

SIN = (-0.16666659712791443, 0.008333083242177963, -0.00019810810044873506, 2.6083068860316416e-06)
COS = (-0.5, 0.04166664183139801, -0.001388839678838849, 2.4761575332377106e-05, -2.607200428883516e-07)


def reduced(u):
    k = jnp.round(u * INV_PI)
    return ((u - k * PI_A) - k * PI_B) - k * PI_C


def sin_of(r, r2):
    return r + r * (r2 * (SIN[0] + r2 * (SIN[1] + r2 * (SIN[2] + r2 * SIN[3]))))


def cos_of(r2):
    return 1.0 + r2 * (COS[0] + r2 * (COS[1] + r2 * (COS[2] + r2 * (COS[3] + r2 * COS[4]))))


def dot(a, b, dims):
    return lax.dot_general(a, b, (dims, ((), ())), preferred_element_type=jnp.float32)


def adam(gradient, master, first_moment, second_moment):
    new_first = 0.9 * first_moment + 0.1 * gradient
    new_second = 0.999 * second_moment + 0.001 * gradient * gradient
    new_master = master - 0.001 * (new_first / BIAS_ONE) / (jnp.sqrt(new_second / BIAS_TWO) + 1e-08)
    return new_master, new_first, new_second


def step_kernel(
    plan,
    clip_hbm, cot_hbm, alpha_hbm, w_hbm, ma_hbm, m1_hbm, m2_hbm,
    ow_hbm, oma_hbm, om1_hbm, om2_hbm,
    clip, cot, alpha_ref, w_lin, w32, w_mat, ma, m1, m2,
    padded, win, hid, bak, d_hid, lhs, grad, pair_buf, xy_buf, acc, z_buf, full, ow, oma, om1, om2,
    in_sem, out_sem, ow_sem, pair_s, pair_r, xy_s, xy_r, zr_s, zr_r, zg_s, zg_r,
    ag_s, ag_r, to_s, to_r,
):
    frames, ch, dp, rep, rows, whole, chunks, parts = plan
    chips = dp // 2
    lin = rows * ch // LANES
    chunk_lin = lin // chunks
    part = chunk_lin // parts
    tall = rows // chunks
    me = lax.axis_index("dp")
    z = lax.axis_index("rep")
    core = me % 2
    g = me // 2
    partner = g * 2 + 1 - core

    loads = [
        pltpu.make_async_copy(s, d, in_sem.at[i])
        for i, (s, d) in enumerate(
            [(alpha_hbm, alpha_ref), (clip_hbm, clip), (w_hbm, w_lin), (cot_hbm, cot), (ma_hbm, ma), (m1_hbm, m1), (m2_hbm, m2)]
        )
    ]
    for c in loads:
        c.start()

    barrier = pltpu.get_barrier_semaphore()
    pl.semaphore_signal(barrier, inc=1, device_id={"dp": partner})
    for k in range(1, chips):
        pl.semaphore_signal(barrier, inc=1, device_id={"dp": (g + k) % chips * 2 + core})
    for k in range(1, rep):
        pl.semaphore_signal(barrier, inc=1, device_id={"rep": (z + k) % rep})

    reach = DILATION * (TAPS // 2)
    base = 16
    split = TAPS * ch

    loads[0].wait()
    loads[1].wait()
    a0 = alpha_ref[0:1, :]
    inv0 = 1.0 / a0
    for h in range(ch // LANES):
        padded[h, 0:base, :] = jnp.zeros((base, LANES), jnp.float32)
        padded[h, base + frames : base + frames + base, :] = jnp.zeros((base, LANES), jnp.float32)

    def activate(c, carry):
        for i in range(2):
            at = pl.multiple_of((2 * c + i) * SLICE, SLICE)
            v = clip[pl.ds(at, SLICE), :].astype(jnp.float32)
            r = reduced(a0 * v)
            s = sin_of(r, r * r)
            first = v + s * s * inv0
            for h in range(ch // LANES):
                padded[h, pl.ds(base + at, SLICE), :] = first[:, h * LANES : (h + 1) * LANES]
        return carry

    lax.fori_loop(0, frames // (2 * SLICE), activate, 0)
    for k in range(TAPS):
        for h in range(ch // LANES):
            start = base + DILATION * k - reach
            win[:, k * ch + h * LANES : k * ch + (h + 1) * LANES] = padded[
                h, start : start + frames, :
            ].astype(jnp.bfloat16)

    loads[2].wait()
    per = ch // LANES
    piece = 256

    def relay(c, carry):
        at = pl.ds(pl.multiple_of(c * piece * per, piece * per), piece * per)
        w32[at, :] = w_lin[at, :].astype(jnp.float32)
        to = pl.ds(pl.multiple_of(c * piece, piece), piece)
        for h in range(per):
            w_mat[to, h * LANES : (h + 1) * LANES] = w32[
                pl.ds(c * piece * per + h, piece, stride=per), :
            ].astype(jnp.bfloat16)
        return carry

    lax.fori_loop(0, (split + ch) // piece, relay, 0)

    loads[3].wait()
    lhs[1] = cot[...].T

    a1 = alpha_ref[1:2, :]
    inv1 = 1.0 / a1
    chunk = 256

    def multiply(c):
        at = slice(c * chunk, (c + 1) * chunk)
        hid[at, :] = dot(win[at, :split], w_mat[:split, :], ((1,), (0,)))
        bak[at, :] = dot(cot[at, :], w_mat[split:, :], ((1,), (1,)))

    multiply(0)
    for c in range(frames // chunk):
        at = slice(c * chunk, (c + 1) * chunk)
        if (c + 1) * chunk < frames:
            multiply(c + 1)
        for i in range(c * chunk, (c + 1) * chunk, SLICE):
            hidden = hid[i : i + SLICE, :]
            r = reduced(a1 * hidden)
            r2 = r * r
            s = sin_of(r, r2)
            win[i : i + SLICE, split : split + ch] = (hidden + s * s * inv1).astype(jnp.bfloat16)
            d_hid[i : i + SLICE, :] = (bak[i : i + SLICE, :] * (1.0 + 2.0 * s * cos_of(r2))).astype(jnp.bfloat16)
        lhs[0, :, at] = d_hid[at, :].T

    def block(b):
        return grad.at[pl.ds(pl.multiple_of(b * rows, rows), rows), :]

    def chunk_rows(b, s):
        return pl.ds(pl.multiple_of(b * rows + s * tall, tall), tall)

    def chunk_of(b, s):
        return grad.at[chunk_rows(b, s), :]

    def tile(t):
        part_of = win[:, pl.ds(pl.multiple_of(t * ch, ch), ch)]
        value = dot(lhs[t // TAPS], part_of, ((1,), (0,)))
        grad[pl.ds(pl.multiple_of(t * ch, ch), ch), :] = value.T

    if not whole:
        lax.fori_loop(0, TAPS + 1, lambda t, c: (tile(t), c)[1], 0)

    pl.semaphore_wait(barrier, chips + rep - 1)

    square = chips == 4

    def neighbour(n, c):
        along, across = g + 1 - 2 * (g % 2), (g + 2) % 4
        if n == 1:
            return along * (1 - c) + across * c
        return along * c + across * (1 - c)

    def chip_at(o, c=core):
        if not square:
            return (g + 1 + o) % chips
        return (3 - g, neighbour(1, c), neighbour(2, c), g)[o]

    def pair_copy(o):
        return pltpu.make_async_remote_copy(
            block(chip_at(o, 1 - core) * 2 + 1 - core), pair_buf.at[o], pair_s.at[o], pair_r.at[o],
            device_id={"dp": partner},
        )

    def xy_copy(s, o):
        to = chip_at(1 if o == 0 else o) if square else chip_at(o)
        return pltpu.make_async_remote_copy(
            chunk_of(chip_at(o) * 2 + core, s), xy_buf.at[s, o], xy_s.at[s, o], xy_r.at[s, o],
            device_id={"dp": to * 2 + core},
        )

    def add_pair(o):
        pair_copy(o).wait_recv()
        b = chip_at(o) * 2 + core
        at = pl.ds(pl.multiple_of(b * rows, rows), rows)
        grad[at, :] = grad[at, :] + pair_buf[o]

    def loop(lo, hi, f):
        if square:
            for j in range(lo, hi):
                f(j)
            return
        lax.fori_loop(lo, hi, lambda j, c: (f(j), c)[1], 0)

    def send_on(o):
        add_pair(o)
        if not square or o < 2:
            xy_copy(0, o).start()

    def second_leg(s):
        if square:
            xy_copy(s, 0).wait_recv()
            at = chunk_rows(chip_at(2) * 2 + core, s)
            grad[at, :] = grad[at, :] + xy_buf[s, 0]
            xy_copy(s, 2).start()

    def z_peer(k):
        return (z + k) % rep

    def part_at(s, q):
        return pl.ds(pl.multiple_of(s * chunk_lin + q * part, part), part)

    def zr_copy(s, k, wait=False):
        if parts > 1:
            src, slot = acc.at[part_at(s, z_peer(k))], k - 1
        else:
            src, slot = acc.at[part_at(s, 0)], (z + rep - k) % rep if wait else z
        return pltpu.make_async_remote_copy(
            src, z_buf.at[s, slot], zr_s.at[s, k - 1], zr_r.at[s, k - 1], device_id={"rep": z_peer(k)},
        )

    def zg_copy(s, k, wait=False):
        at = part_at(s, (z + rep - k) % rep if wait else z)
        return pltpu.make_async_remote_copy(
            full.at[at], full.at[at], zg_s.at[s, k - 1], zg_r.at[s, k - 1], device_id={"rep": z_peer(k)},
        )

    def sum_chips(s):
        def add_chip(o, total):
            xy_copy(s, o).wait_recv()
            return total + xy_buf[s, o]

        total = grad[chunk_rows(me, s), :]
        if square:
            total = add_chip(2, add_chip(1, total))
        else:
            total = lax.fori_loop(0, chips - 1, add_chip, total)
        for h in range(per):
            acc[pl.ds(s * chunk_lin + h, chunk_lin // per, stride=per), :] = total[:, h * LANES : (h + 1) * LANES]
        for k in range(1, rep):
            zr_copy(s, k).start()

    def sum_replicas(s):
        if parts > 1:
            own = acc[part_at(s, z), :]
            for k in range(1, rep):
                zr_copy(s, k, True).wait_recv()
                own = own + z_buf[s, k - 1]
            full[part_at(s, z), :] = own
            for k in range(1, rep):
                zg_copy(s, k).start()
        else:
            z_buf[s, z] = acc[part_at(s, 0), :]
            for k in range(1, rep):
                zr_copy(s, k, True).wait_recv()
            own = z_buf[s, 0]
            for k in range(1, rep):
                own = own + z_buf[s, k]
            full[part_at(s, 0), :] = own

    def lin_at(s, owner=0):
        return pl.ds(pl.multiple_of(owner * lin + s * chunk_lin, chunk_lin), chunk_lin)

    def place(owner, s):
        return ow.at[lin_at(s, owner), :]

    def source(j, c=core):
        if not square:
            return (g + chips - j) % chips
        return (g, neighbour(1, c), neighbour(2, c), 3 - g)[j]

    def ag_copy(s, j, wait=False):
        if square:
            to = neighbour(1 if j == 1 else 2, core)
            sent = neighbour(1, core) if j == 3 else g
        else:
            to, sent = (g + j) % chips, g
        at = place((source(j) if wait else sent) * 2 + core, s)
        return pltpu.make_async_remote_copy(
            at, at, ag_s.at[s, j], ag_r.at[s, j], device_id={"dp": to * 2 + core},
        )

    def to_copy(s, j, wait=False):
        c = 1 - core if wait else core
        at = place(source(j, c) * 2 + c, s)
        return pltpu.make_async_remote_copy(
            at, at, to_s.at[s, j], to_r.at[s, j], device_id={"dp": partner},
        )

    def ow_copy(s, b):
        at = lin_at(s, b)
        return pltpu.make_async_copy(ow.at[at, :], ow_hbm.at[at, :], ow_sem.at[s, b])

    def outs(s):
        at = lin_at(s)
        return [
            pltpu.make_async_copy(src.at[at, :], dst.at[at, :], out_sem.at[s, i])
            for i, (src, dst) in enumerate([(oma, oma_hbm), (om1, om1_hbm), (om2, om2_hbm)])
        ]

    direct = 3 if square else chips

    def update(s):
        if parts > 1:
            for k in range(1, rep):
                zg_copy(s, k, True).wait_recv()
        at = lin_at(s)
        new_master, new_first, new_second = adam(full[at, :], ma[at, :], m1[at, :], m2[at, :])
        ow[lin_at(s, me), :] = new_master.astype(jnp.bfloat16)
        loop(1, direct, lambda j: ag_copy(s, j).start())
        to_copy(s, 0).start()
        oma[at, :] = new_master
        om1[at, :] = new_first
        om2[at, :] = new_second
        for c in outs(s):
            c.start()

    def take(s, j):
        ag_copy(s, j, True).wait_recv()
        to_copy(s, j).start()

    def hand_on(s):
        if square:
            ag_copy(s, 1, True).wait_recv()
            ag_copy(s, 3).start()
            to_copy(s, 1).start()
            take(s, 2)
        else:
            loop(1, chips, lambda j: take(s, j))

    def hand_on_last(s):
        if square:
            take(s, 3)

    def store(s):
        loop(0, chips, lambda j: to_copy(s, j, True).wait_recv())
        loop(0, dp, lambda b: ow_copy(s, b).start())

    def follow(s):
        def one(o):
            xy_copy(s - 1, o).wait_send()
            xy_copy(s, o).start()

        loop(0, 2 if square else chips - 1, one)

    def produce(o):
        if whole:
            tile(chip_at(o, 1 - core) * 2 + 1 - core)
        pair_copy(o).start()
        if whole:
            tile(chip_at(o) * 2 + core)

    def produce_and_send(o):
        produce(o)
        send_on(o - 1)

    produce(0)
    loop(1, chips, produce_and_send)
    add_pair(chips - 1)
    for c in loads[4:]:
        c.wait()
    stages = (second_leg, sum_chips, sum_replicas, update, hand_on, hand_on_last, store)
    for t in range(chunks + len(stages) - 1):
        if 0 < t + 1 < chunks:
            follow(t + 1)
        for late, stage in enumerate(stages):
            if 0 <= t - late < chunks:
                stage(t - late)

    loop(0, chips, lambda o: pair_copy(o).wait_send())
    loop(0, chips - 1, lambda o: xy_copy(chunks - 1, o).wait_send())
    for s in range(chunks):
        if square and s < chunks - 1:
            xy_copy(s, 2).wait_send()
        for k in range(1, rep):
            zr_copy(s, k).wait_send()
            if parts > 1:
                zg_copy(s, k).wait_send()
        loop(1, chips, lambda j: ag_copy(s, j).wait_send())
        loop(0, chips, lambda j: to_copy(s, j).wait_send())
        loop(0, dp, lambda b: ow_copy(s, b).wait())
        for c in outs(s):
            c.wait()


def results_kernel(*refs):
    n = len(refs) // 3
    ins, outs, held, (in_sem, out_sem) = refs[:n], refs[n : 2 * n], refs[2 * n : 3 * n], refs[3 * n :]
    loads, stores = [], []
    for i in range(n):
        size = ins[i].shape[0] // PIECES
        for p in range(PIECES):
            at = pl.ds(p * size, size)
            loads.append(pltpu.make_async_copy(ins[i].at[at, :], held[i].at[at, :], in_sem.at[i, p]))
            stores.append(pltpu.make_async_copy(held[i].at[at, :], outs[i].at[at, :], out_sem.at[i, p]))
    for c in loads:
        c.start()
    for load, store in zip(loads, stores):
        load.wait()
        store.start()
    for c in stores:
        c.wait()


def shards(dp, rep, clips, cotangent, alphas, weights, master, first_moment, second_moment):
    frames, ch = clips.shape[1:]
    params = weights.shape[0]
    own = master.shape[0]
    rows = own // ch
    lin = own // LANES
    chips = dp // 2
    whole = rows == ch
    chunks = CHUNKS if whole else 1
    parts = rep if lin // chunks % (16 * rep) == 0 else 1
    part = lin // chunks // parts
    plan = (frames, ch, dp, rep, rows, whole, chunks, parts)
    anywhere = pl.BlockSpec(memory_space=pl.ANY)
    f32, bf16 = jnp.float32, jnp.bfloat16
    dma = pltpu.SemaphoreType.DMA
    outs = pl.pallas_call(
        functools.partial(step_kernel, plan),
        out_shape=(
            jax.ShapeDtypeStruct((params // LANES, LANES), bf16),
            jax.ShapeDtypeStruct((lin, LANES), f32),
            jax.ShapeDtypeStruct((lin, LANES), f32),
            jax.ShapeDtypeStruct((lin, LANES), f32),
        ),
        in_specs=[anywhere] * 7,
        out_specs=(anywhere,) * 4,
        scratch_shapes=[
            pltpu.VMEM((frames, ch), bf16),
            pltpu.VMEM((frames, ch), bf16),
            pltpu.VMEM(alphas.shape, f32),
            pltpu.VMEM((params // LANES, LANES), bf16),
            pltpu.VMEM((params // LANES, LANES), f32),
            pltpu.VMEM((params // ch, ch), bf16),
            pltpu.VMEM((lin, LANES), f32),
            pltpu.VMEM((lin, LANES), f32),
            pltpu.VMEM((lin, LANES), f32),
            pltpu.VMEM((ch // LANES, frames + 32, LANES), f32),
            pltpu.VMEM((frames, (TAPS + 1) * ch), bf16),
            pltpu.VMEM((frames, ch), f32),
            pltpu.VMEM((frames, ch), f32),
            pltpu.VMEM((frames, ch), bf16),
            pltpu.VMEM((2, ch, frames), bf16),
            pltpu.VMEM((params // ch, ch), f32),
            pltpu.VMEM((chips, rows, ch), f32),
            pltpu.VMEM((chunks, chips - 1, rows // chunks, ch), f32),
            pltpu.VMEM((lin, LANES), f32),
            pltpu.VMEM((chunks, rep, part, LANES), f32),
            pltpu.VMEM((lin, LANES), f32),
            pltpu.VMEM((params // LANES, LANES), bf16),
            pltpu.VMEM((lin, LANES), f32),
            pltpu.VMEM((lin, LANES), f32),
            pltpu.VMEM((lin, LANES), f32),
            dma((7,)),
            dma((chunks, 3)),
            dma((chunks, dp)),
            dma((chips,)), dma((chips,)),
            dma((chunks, chips)), dma((chunks, chips)),
            dma((chunks, rep)), dma((chunks, rep)),
            dma((chunks, rep)), dma((chunks, rep)),
            dma((chunks, chips)), dma((chunks, chips)),
            dma((chunks, chips)), dma((chunks, chips)),
        ],
        compiler_params=pltpu.CompilerParams(
            collective_id=0, has_side_effects=True, vmem_limit_bytes=64 * 1024 * 1024
        ),
        name="train_step",
    )(
        clips[0],
        cotangent[0],
        alphas,
        weights.reshape(params // LANES, LANES),
        master.reshape(lin, LANES),
        first_moment.reshape(lin, LANES),
        second_moment.reshape(lin, LANES),
    )
    outs = pl.pallas_call(
        results_kernel,
        out_shape=tuple(jax.ShapeDtypeStruct(o.shape, o.dtype) for o in outs),
        in_specs=[anywhere] * len(outs),
        out_specs=(anywhere,) * len(outs),
        scratch_shapes=[pltpu.VMEM(o.shape, o.dtype) for o in outs] + [dma((len(outs), PIECES))] * 2,
        compiler_params=pltpu.CompilerParams(vmem_limit_bytes=64 * 1024 * 1024),
        name="results",
    )(*outs)
    return tuple(o.reshape(-1) for o in outs)


def solution(mesh):
    return jax.shard_map(
        functools.partial(shards, mesh.shape["dp"], mesh.shape["rep"]),
        mesh=mesh,
        in_specs=(
            P(("dp", "rep"), None, None),
            P(("dp", "rep"), None, None),
            P(),
            P(),
            P("dp"),
            P("dp"),
            P("dp"),
        ),
        out_specs=(P(), P("dp"), P("dp"), P("dp")),
        check_vma=False,
    )
```

```python
import functools

import jax
import jax.numpy as jnp
from jax import lax
from jax.experimental import pallas as pl
from jax.experimental.pallas import tpu as pltpu
from jax.sharding import PartitionSpec as P

TAPS = 7
DILATION = 3
LANES = 128
SLICE = 32
PIECES = 2
CHUNKS = 2

BIAS_ONE = 0.9999734386011124
BIAS_TWO = 0.09520785288629041

PI_A = 3.140625
PI_B = 9.67502593994140625e-4
PI_C = 1.509957990978376432e-7
INV_PI = 0.3183098861837907

SIN = (-0.16666659712791443, 0.008333083242177963, -0.00019810810044873506, 2.6083068860316416e-06)
COS = (-0.5, 0.04166664183139801, -0.001388839678838849, 2.4761575332377106e-05, -2.607200428883516e-07)


def reduced(u):
    k = jnp.round(u * INV_PI)
    return ((u - k * PI_A) - k * PI_B) - k * PI_C


def sin_of(r, r2):
    return r + r * (r2 * (SIN[0] + r2 * (SIN[1] + r2 * (SIN[2] + r2 * SIN[3]))))


def cos_of(r2):
    return 1.0 + r2 * (COS[0] + r2 * (COS[1] + r2 * (COS[2] + r2 * (COS[3] + r2 * COS[4]))))


def dot(a, b, dims):
    return lax.dot_general(a, b, (dims, ((), ())), preferred_element_type=jnp.float32)


def adam(gradient, master, first_moment, second_moment):
    new_first = 0.9 * first_moment + 0.1 * gradient
    new_second = 0.999 * second_moment + 0.001 * gradient * gradient
    new_master = master - 0.001 * (new_first / BIAS_ONE) / (jnp.sqrt(new_second / BIAS_TWO) + 1e-08)
    return new_master, new_first, new_second


def step_kernel(
    plan,
    clip_hbm, cot_hbm, alpha_hbm, w_hbm, ma_hbm, m1_hbm, m2_hbm,
    ow_hbm, oma_hbm, om1_hbm, om2_hbm,
    clip, cot, alpha_ref, w_lin, w32, w_mat, ma, m1, m2,
    padded, win, hid, bak, d_hid, lhs, grad, pair_buf, xy_buf, acc, z_buf, full, ow, oma, om1, om2,
    in_sem, out_sem, ow_sem, pair_s, pair_r, xy_s, xy_r, zr_s, zr_r, zg_s, zg_r,
    ag_s, ag_r, to_s, to_r,
):
    frames, ch, dp, rep, rows, whole, chunks, parts = plan
    chips = dp // 2
    lin = rows * ch // LANES
    chunk_lin = lin // chunks
    part = chunk_lin // parts
    tall = rows // chunks
    me = lax.axis_index("dp")
    z = lax.axis_index("rep")
    core = me % 2
    g = me // 2
    partner = g * 2 + 1 - core

    loads = [
        pltpu.make_async_copy(s, d, in_sem.at[i])
        for i, (s, d) in enumerate(
            [(alpha_hbm, alpha_ref), (clip_hbm, clip), (w_hbm, w_lin), (cot_hbm, cot), (ma_hbm, ma), (m1_hbm, m1), (m2_hbm, m2)]
        )
    ]
    for c in loads:
        c.start()

    barrier = pltpu.get_barrier_semaphore()
    pl.semaphore_signal(barrier, inc=1, device_id={"dp": partner})
    for k in range(1, chips):
        pl.semaphore_signal(barrier, inc=1, device_id={"dp": (g + k) % chips * 2 + core})
    for k in range(1, rep):
        pl.semaphore_signal(barrier, inc=1, device_id={"rep": (z + k) % rep})

    reach = DILATION * (TAPS // 2)
    base = 16
    split = TAPS * ch

    loads[0].wait()
    loads[1].wait()
    a0 = alpha_ref[0:1, :]
    inv0 = 1.0 / a0
    for h in range(ch // LANES):
        padded[h, 0:base, :] = jnp.zeros((base, LANES), jnp.float32)
        padded[h, base + frames : base + frames + base, :] = jnp.zeros((base, LANES), jnp.float32)

    def activate(c, carry):
        for i in range(2):
            at = pl.multiple_of((2 * c + i) * SLICE, SLICE)
            v = clip[pl.ds(at, SLICE), :].astype(jnp.float32)
            r = reduced(a0 * v)
            s = sin_of(r, r * r)
            first = v + s * s * inv0
            for h in range(ch // LANES):
                padded[h, pl.ds(base + at, SLICE), :] = first[:, h * LANES : (h + 1) * LANES]
        return carry

    lax.fori_loop(0, frames // (2 * SLICE), activate, 0)
    for k in range(TAPS):
        for h in range(ch // LANES):
            start = base + DILATION * k - reach
            win[:, k * ch + h * LANES : k * ch + (h + 1) * LANES] = padded[
                h, start : start + frames, :
            ].astype(jnp.bfloat16)

    loads[2].wait()
    per = ch // LANES
    piece = 256

    def relay(c, carry):
        at = pl.ds(pl.multiple_of(c * piece * per, piece * per), piece * per)
        w32[at, :] = w_lin[at, :].astype(jnp.float32)
        to = pl.ds(pl.multiple_of(c * piece, piece), piece)
        for h in range(per):
            w_mat[to, h * LANES : (h + 1) * LANES] = w32[
                pl.ds(c * piece * per + h, piece, stride=per), :
            ].astype(jnp.bfloat16)
        return carry

    lax.fori_loop(0, (split + ch) // piece, relay, 0)

    loads[3].wait()
    lhs[1] = cot[...].T

    a1 = alpha_ref[1:2, :]
    inv1 = 1.0 / a1
    chunk = 256

    def multiply(c):
        at = slice(c * chunk, (c + 1) * chunk)
        hid[at, :] = dot(win[at, :split], w_mat[:split, :], ((1,), (0,)))
        bak[at, :] = dot(cot[at, :], w_mat[split:, :], ((1,), (1,)))

    multiply(0)
    for c in range(frames // chunk):
        at = slice(c * chunk, (c + 1) * chunk)
        if (c + 1) * chunk < frames:
            multiply(c + 1)
        for i in range(c * chunk, (c + 1) * chunk, SLICE):
            hidden = hid[i : i + SLICE, :]
            r = reduced(a1 * hidden)
            r2 = r * r
            s = sin_of(r, r2)
            win[i : i + SLICE, split : split + ch] = (hidden + s * s * inv1).astype(jnp.bfloat16)
            d_hid[i : i + SLICE, :] = (bak[i : i + SLICE, :] * (1.0 + 2.0 * s * cos_of(r2))).astype(jnp.bfloat16)
        lhs[0, :, at] = d_hid[at, :].T

    def block(b):
        return grad.at[pl.ds(pl.multiple_of(b * rows, rows), rows), :]

    def chunk_rows(b, s):
        return pl.ds(pl.multiple_of(b * rows + s * tall, tall), tall)

    def chunk_of(b, s):
        return grad.at[chunk_rows(b, s), :]

    def tile(t):
        part_of = win[:, pl.ds(pl.multiple_of(t * ch, ch), ch)]
        value = dot(lhs[t // TAPS], part_of, ((1,), (0,)))
        grad[pl.ds(pl.multiple_of(t * ch, ch), ch), :] = value.T

    if not whole:
        lax.fori_loop(0, TAPS + 1, lambda t, c: (tile(t), c)[1], 0)

    pl.semaphore_wait(barrier, chips + rep - 1)

    def chip_at(o):
        return (g + 1 + o) % chips

    def pair_copy(o):
        return pltpu.make_async_remote_copy(
            block(chip_at(o) * 2 + 1 - core), pair_buf.at[o], pair_s.at[o], pair_r.at[o],
            device_id={"dp": partner},
        )

    def xy_copy(s, o):
        to = chip_at(o)
        return pltpu.make_async_remote_copy(
            chunk_of(to * 2 + core, s), xy_buf.at[s, o], xy_s.at[s, o], xy_r.at[s, o],
            device_id={"dp": to * 2 + core},
        )

    def add_pair(o):
        pair_copy(o).wait_recv()
        b = chip_at(o) * 2 + core
        at = pl.ds(pl.multiple_of(b * rows, rows), rows)
        grad[at, :] = grad[at, :] + pair_buf[o]

    def loop(lo, hi, f):
        lax.fori_loop(lo, hi, lambda j, c: (f(j), c)[1], 0)

    def send_on(o):
        add_pair(o)
        for s in range(chunks):
            xy_copy(s, o).start()

    def z_peer(k):
        return (z + k) % rep

    def part_at(s, q):
        return pl.ds(pl.multiple_of(s * chunk_lin + q * part, part), part)

    def zr_copy(s, k, wait=False):
        if parts > 1:
            src, slot = acc.at[part_at(s, z_peer(k))], k - 1
        else:
            src, slot = acc.at[part_at(s, 0)], (z + rep - k) % rep if wait else z
        return pltpu.make_async_remote_copy(
            src, z_buf.at[s, slot], zr_s.at[s, k - 1], zr_r.at[s, k - 1], device_id={"rep": z_peer(k)},
        )

    def zg_copy(s, k, wait=False):
        at = part_at(s, (z + rep - k) % rep if wait else z)
        return pltpu.make_async_remote_copy(
            full.at[at], full.at[at], zg_s.at[s, k - 1], zg_r.at[s, k - 1], device_id={"rep": z_peer(k)},
        )

    def sum_chips(s):
        def add_chip(o, total):
            xy_copy(s, o).wait_recv()
            return total + xy_buf[s, o]

        total = lax.fori_loop(0, chips - 1, add_chip, grad[chunk_rows(me, s), :])
        for h in range(per):
            acc[pl.ds(s * chunk_lin + h, chunk_lin // per, stride=per), :] = total[:, h * LANES : (h + 1) * LANES]
        for k in range(1, rep):
            zr_copy(s, k).start()

    def sum_replicas(s):
        if parts > 1:
            own = acc[part_at(s, z), :]
            for k in range(1, rep):
                zr_copy(s, k, True).wait_recv()
                own = own + z_buf[s, k - 1]
            full[part_at(s, z), :] = own
            for k in range(1, rep):
                zg_copy(s, k).start()
        else:
            z_buf[s, z] = acc[part_at(s, 0), :]
            for k in range(1, rep):
                zr_copy(s, k, True).wait_recv()
            own = z_buf[s, 0]
            for k in range(1, rep):
                own = own + z_buf[s, k]
            full[part_at(s, 0), :] = own

    def lin_at(s, owner=0):
        return pl.ds(pl.multiple_of(owner * lin + s * chunk_lin, chunk_lin), chunk_lin)

    def place(owner, s):
        return ow.at[lin_at(s, owner), :]

    def ag_copy(s, j, wait=False):
        at = place((g + chips - j) % chips * 2 + core if wait else me, s)
        return pltpu.make_async_remote_copy(
            at, at, ag_s.at[s, j], ag_r.at[s, j], device_id={"dp": (g + j) % chips * 2 + core},
        )

    def to_copy(s, j, wait=False):
        at = place((g + chips - j) % chips * 2 + (1 - core if wait else core), s)
        return pltpu.make_async_remote_copy(
            at, at, to_s.at[s, j], to_r.at[s, j], device_id={"dp": partner},
        )

    def ow_copy(s, b):
        at = lin_at(s, b)
        return pltpu.make_async_copy(ow.at[at, :], ow_hbm.at[at, :], ow_sem.at[s, b])

    def outs(s):
        at = lin_at(s)
        return [
            pltpu.make_async_copy(src.at[at, :], dst.at[at, :], out_sem.at[s, i])
            for i, (src, dst) in enumerate([(oma, oma_hbm), (om1, om1_hbm), (om2, om2_hbm)])
        ]

    def update(s):
        if parts > 1:
            for k in range(1, rep):
                zg_copy(s, k, True).wait_recv()
        at = lin_at(s)
        new_master, new_first, new_second = adam(full[at, :], ma[at, :], m1[at, :], m2[at, :])
        ow[lin_at(s, me), :] = new_master.astype(jnp.bfloat16)
        loop(1, chips, lambda j: ag_copy(s, j).start())
        to_copy(s, 0).start()
        oma[at, :] = new_master
        om1[at, :] = new_first
        om2[at, :] = new_second
        for c in outs(s):
            c.start()

    def hand_on(s):
        def one(j):
            ag_copy(s, j, True).wait_recv()
            to_copy(s, j).start()

        loop(1, chips, one)

    def store(s):
        loop(0, chips, lambda j: to_copy(s, j, True).wait_recv())
        loop(0, dp, lambda b: ow_copy(s, b).start())

    def produce(o):
        i = chip_at(o)
        if whole:
            tile(i * 2 + 1 - core)
        pair_copy(o).start()
        if whole:
            tile(i * 2 + core)

    def produce_and_send(o):
        produce(o)
        send_on(o - 1)

    produce(0)
    loop(1, chips, produce_and_send)
    add_pair(chips - 1)
    for c in loads[4:]:
        c.wait()
    for t in range(chunks + 4):
        for late, stage in enumerate((sum_chips, sum_replicas, update, hand_on, store)):
            if 0 <= t - late < chunks:
                stage(t - late)

    loop(0, chips, lambda o: pair_copy(o).wait_send())
    for s in range(chunks):
        loop(0, chips - 1, lambda o: xy_copy(s, o).wait_send())
        for k in range(1, rep):
            zr_copy(s, k).wait_send()
            if parts > 1:
                zg_copy(s, k).wait_send()
        loop(1, chips, lambda j: ag_copy(s, j).wait_send())
        loop(0, chips, lambda j: to_copy(s, j).wait_send())
        loop(0, dp, lambda b: ow_copy(s, b).wait())
        for c in outs(s):
            c.wait()


def results_kernel(*refs):
    n = len(refs) // 3
    ins, outs, held, (in_sem, out_sem) = refs[:n], refs[n : 2 * n], refs[2 * n : 3 * n], refs[3 * n :]
    loads, stores = [], []
    for i in range(n):
        size = ins[i].shape[0] // PIECES
        for p in range(PIECES):
            at = pl.ds(p * size, size)
            loads.append(pltpu.make_async_copy(ins[i].at[at, :], held[i].at[at, :], in_sem.at[i, p]))
            stores.append(pltpu.make_async_copy(held[i].at[at, :], outs[i].at[at, :], out_sem.at[i, p]))
    for c in loads:
        c.start()
    for load, store in zip(loads, stores):
        load.wait()
        store.start()
    for c in stores:
        c.wait()


def shards(dp, rep, clips, cotangent, alphas, weights, master, first_moment, second_moment):
    frames, ch = clips.shape[1:]
    params = weights.shape[0]
    own = master.shape[0]
    rows = own // ch
    lin = own // LANES
    chips = dp // 2
    whole = rows == ch
    chunks = CHUNKS if whole else 1
    parts = rep if lin // chunks % (16 * rep) == 0 else 1
    part = lin // chunks // parts
    plan = (frames, ch, dp, rep, rows, whole, chunks, parts)
    anywhere = pl.BlockSpec(memory_space=pl.ANY)
    f32, bf16 = jnp.float32, jnp.bfloat16
    dma = pltpu.SemaphoreType.DMA
    outs = pl.pallas_call(
        functools.partial(step_kernel, plan),
        out_shape=(
            jax.ShapeDtypeStruct((params // LANES, LANES), bf16),
            jax.ShapeDtypeStruct((lin, LANES), f32),
            jax.ShapeDtypeStruct((lin, LANES), f32),
            jax.ShapeDtypeStruct((lin, LANES), f32),
        ),
        in_specs=[anywhere] * 7,
        out_specs=(anywhere,) * 4,
        scratch_shapes=[
            pltpu.VMEM((frames, ch), bf16),
            pltpu.VMEM((frames, ch), bf16),
            pltpu.VMEM(alphas.shape, f32),
            pltpu.VMEM((params // LANES, LANES), bf16),
            pltpu.VMEM((params // LANES, LANES), f32),
            pltpu.VMEM((params // ch, ch), bf16),
            pltpu.VMEM((lin, LANES), f32),
            pltpu.VMEM((lin, LANES), f32),
            pltpu.VMEM((lin, LANES), f32),
            pltpu.VMEM((ch // LANES, frames + 32, LANES), f32),
            pltpu.VMEM((frames, (TAPS + 1) * ch), bf16),
            pltpu.VMEM((frames, ch), f32),
            pltpu.VMEM((frames, ch), f32),
            pltpu.VMEM((frames, ch), bf16),
            pltpu.VMEM((2, ch, frames), bf16),
            pltpu.VMEM((params // ch, ch), f32),
            pltpu.VMEM((chips, rows, ch), f32),
            pltpu.VMEM((chunks, chips - 1, rows // chunks, ch), f32),
            pltpu.VMEM((lin, LANES), f32),
            pltpu.VMEM((chunks, rep, part, LANES), f32),
            pltpu.VMEM((lin, LANES), f32),
            pltpu.VMEM((params // LANES, LANES), bf16),
            pltpu.VMEM((lin, LANES), f32),
            pltpu.VMEM((lin, LANES), f32),
            pltpu.VMEM((lin, LANES), f32),
            dma((7,)),
            dma((chunks, 3)),
            dma((chunks, dp)),
            dma((chips,)), dma((chips,)),
            dma((chunks, chips)), dma((chunks, chips)),
            dma((chunks, rep)), dma((chunks, rep)),
            dma((chunks, rep)), dma((chunks, rep)),
            dma((chunks, chips)), dma((chunks, chips)),
            dma((chunks, chips)), dma((chunks, chips)),
        ],
        compiler_params=pltpu.CompilerParams(
            collective_id=0, has_side_effects=True, vmem_limit_bytes=64 * 1024 * 1024
        ),
        name="train_step",
    )(
        clips[0],
        cotangent[0],
        alphas,
        weights.reshape(params // LANES, LANES),
        master.reshape(lin, LANES),
        first_moment.reshape(lin, LANES),
        second_moment.reshape(lin, LANES),
    )
    outs = pl.pallas_call(
        results_kernel,
        out_shape=tuple(jax.ShapeDtypeStruct(o.shape, o.dtype) for o in outs),
        in_specs=[anywhere] * len(outs),
        out_specs=(anywhere,) * len(outs),
        scratch_shapes=[pltpu.VMEM(o.shape, o.dtype) for o in outs] + [dma((len(outs), PIECES))] * 2,
        compiler_params=pltpu.CompilerParams(vmem_limit_bytes=64 * 1024 * 1024),
        name="results",
    )(*outs)
    return tuple(o.reshape(-1) for o in outs)


def solution(mesh):
    return jax.shard_map(
        functools.partial(shards, mesh.shape["dp"], mesh.shape["rep"]),
        mesh=mesh,
        in_specs=(
            P(("dp", "rep"), None, None),
            P(("dp", "rep"), None, None),
            P(),
            P(),
            P("dp"),
            P("dp"),
            P("dp"),
        ),
        out_specs=(P(), P("dp"), P("dp"), P("dp")),
        check_vma=False,
    )
```

```python
import functools

import jax
import jax.numpy as jnp
from jax import lax
from jax.experimental import pallas as pl
from jax.experimental.pallas import tpu as pltpu
from jax.sharding import PartitionSpec as P

TAPS = 7
DILATION = 3
LANES = 128
SLICE = 32
PIECES = 4
CHUNKS = 4

BIAS_ONE = 0.9999734386011124
BIAS_TWO = 0.09520785288629041

PI_A = 3.140625
PI_B = 9.67502593994140625e-4
PI_C = 1.509957990978376432e-7
INV_PI = 0.3183098861837907

SIN = (-0.16666659712791443, 0.008333083242177963, -0.00019810810044873506, 2.6083068860316416e-06)
COS = (-0.5, 0.04166664183139801, -0.001388839678838849, 2.4761575332377106e-05, -2.607200428883516e-07)


def reduced(u):
    k = jnp.round(u * INV_PI)
    return ((u - k * PI_A) - k * PI_B) - k * PI_C


def sin_of(r, r2):
    return r + r * (r2 * (SIN[0] + r2 * (SIN[1] + r2 * (SIN[2] + r2 * SIN[3]))))


def cos_of(r2):
    return 1.0 + r2 * (COS[0] + r2 * (COS[1] + r2 * (COS[2] + r2 * (COS[3] + r2 * COS[4]))))


def dot(a, b, dims):
    return lax.dot_general(a, b, (dims, ((), ())), preferred_element_type=jnp.float32)


def adam(gradient, master, first_moment, second_moment):
    new_first = 0.9 * first_moment + 0.1 * gradient
    new_second = 0.999 * second_moment + 0.001 * gradient * gradient
    new_master = master - 0.001 * (new_first / BIAS_ONE) / (jnp.sqrt(new_second / BIAS_TWO) + 1e-08)
    return new_master, new_first, new_second


def step_kernel(
    plan,
    clip_hbm, cot_hbm, alpha_hbm, w_hbm, ma_hbm, m1_hbm, m2_hbm,
    ow_hbm, oma_hbm, om1_hbm, om2_hbm,
    clip, cot, alpha_ref, w_lin, w32, w_mat, ma, m1, m2,
    padded, win, hid, bak, d_hid, lhs, grad, pair_buf, xy_buf, acc, z_buf, full, ow, oma, om1, om2,
    in_sem, out_sem, ow_sem, pair_s, pair_r, xy_s, xy_r, zr_s, zr_r, zg_s, zg_r,
    ag_s, ag_r, to_s, to_r,
):
    frames, ch, dp, rep, rows, whole, chunks, parts = plan
    chips = dp // 2
    lin = rows * ch // LANES
    chunk_lin = lin // chunks
    part = chunk_lin // parts
    tall = rows // chunks
    me = lax.axis_index("dp")
    z = lax.axis_index("rep")
    core = me % 2
    g = me // 2
    partner = g * 2 + 1 - core

    loads = [
        pltpu.make_async_copy(s, d, in_sem.at[i])
        for i, (s, d) in enumerate(
            [(alpha_hbm, alpha_ref), (clip_hbm, clip), (w_hbm, w_lin), (cot_hbm, cot), (ma_hbm, ma), (m1_hbm, m1), (m2_hbm, m2)]
        )
    ]
    for c in loads:
        c.start()

    barrier = pltpu.get_barrier_semaphore()
    pl.semaphore_signal(barrier, inc=1, device_id={"dp": partner})
    for k in range(1, chips):
        pl.semaphore_signal(barrier, inc=1, device_id={"dp": (g + k) % chips * 2 + core})
    for k in range(1, rep):
        pl.semaphore_signal(barrier, inc=1, device_id={"rep": (z + k) % rep})

    reach = DILATION * (TAPS // 2)
    base = 16
    split = TAPS * ch

    loads[0].wait()
    loads[1].wait()
    a0 = alpha_ref[0:1, :]
    inv0 = 1.0 / a0
    for h in range(ch // LANES):
        padded[h, 0:base, :] = jnp.zeros((base, LANES), jnp.float32)
        padded[h, base + frames : base + frames + base, :] = jnp.zeros((base, LANES), jnp.float32)

    def activate(c, carry):
        for i in range(2):
            at = pl.multiple_of((2 * c + i) * SLICE, SLICE)
            v = clip[pl.ds(at, SLICE), :].astype(jnp.float32)
            r = reduced(a0 * v)
            s = sin_of(r, r * r)
            first = v + s * s * inv0
            for h in range(ch // LANES):
                padded[h, pl.ds(base + at, SLICE), :] = first[:, h * LANES : (h + 1) * LANES]
        return carry

    lax.fori_loop(0, frames // (2 * SLICE), activate, 0)
    for k in range(TAPS):
        for h in range(ch // LANES):
            start = base + DILATION * k - reach
            win[:, k * ch + h * LANES : k * ch + (h + 1) * LANES] = padded[
                h, start : start + frames, :
            ].astype(jnp.bfloat16)

    loads[2].wait()
    per = ch // LANES
    piece = 256

    def relay(c, carry):
        at = pl.ds(pl.multiple_of(c * piece * per, piece * per), piece * per)
        w32[at, :] = w_lin[at, :].astype(jnp.float32)
        to = pl.ds(pl.multiple_of(c * piece, piece), piece)
        for h in range(per):
            w_mat[to, h * LANES : (h + 1) * LANES] = w32[
                pl.ds(c * piece * per + h, piece, stride=per), :
            ].astype(jnp.bfloat16)
        return carry

    lax.fori_loop(0, (split + ch) // piece, relay, 0)

    loads[3].wait()
    lhs[1] = cot[...].T

    a1 = alpha_ref[1:2, :]
    inv1 = 1.0 / a1
    chunk = 256

    def multiply(c):
        at = slice(c * chunk, (c + 1) * chunk)
        hid[at, :] = dot(win[at, :split], w_mat[:split, :], ((1,), (0,)))
        bak[at, :] = dot(cot[at, :], w_mat[split:, :], ((1,), (1,)))

    multiply(0)
    for c in range(frames // chunk):
        at = slice(c * chunk, (c + 1) * chunk)
        if (c + 1) * chunk < frames:
            multiply(c + 1)
        for i in range(c * chunk, (c + 1) * chunk, SLICE):
            hidden = hid[i : i + SLICE, :]
            r = reduced(a1 * hidden)
            r2 = r * r
            s = sin_of(r, r2)
            win[i : i + SLICE, split : split + ch] = (hidden + s * s * inv1).astype(jnp.bfloat16)
            d_hid[i : i + SLICE, :] = (bak[i : i + SLICE, :] * (1.0 + 2.0 * s * cos_of(r2))).astype(jnp.bfloat16)
        lhs[0, :, at] = d_hid[at, :].T

    def block(b):
        return grad.at[pl.ds(pl.multiple_of(b * rows, rows), rows), :]

    def chunk_rows(b, s):
        return pl.ds(pl.multiple_of(b * rows + s * tall, tall), tall)

    def chunk_of(b, s):
        return grad.at[chunk_rows(b, s), :]

    def tile(t):
        part_of = win[:, pl.ds(pl.multiple_of(t * ch, ch), ch)]
        value = dot(lhs[t // TAPS], part_of, ((1,), (0,)))
        grad[pl.ds(pl.multiple_of(t * ch, ch), ch), :] = value.T

    if not whole:
        lax.fori_loop(0, TAPS + 1, lambda t, c: (tile(t), c)[1], 0)

    pl.semaphore_wait(barrier, chips + rep - 1)

    def chip_at(o):
        return (g + 1 + o) % chips

    def pair_copy(o):
        return pltpu.make_async_remote_copy(
            block(chip_at(o) * 2 + 1 - core), pair_buf.at[o], pair_s.at[o], pair_r.at[o],
            device_id={"dp": partner},
        )

    def xy_copy(s, o):
        to = chip_at(o)
        return pltpu.make_async_remote_copy(
            chunk_of(to * 2 + core, s), xy_buf.at[s, o], xy_s.at[s, o], xy_r.at[s, o],
            device_id={"dp": to * 2 + core},
        )

    def add_pair(o):
        pair_copy(o).wait_recv()
        b = chip_at(o) * 2 + core
        at = pl.ds(pl.multiple_of(b * rows, rows), rows)
        grad[at, :] = grad[at, :] + pair_buf[o]

    def loop(lo, hi, f):
        lax.fori_loop(lo, hi, lambda j, c: (f(j), c)[1], 0)

    def send_on(o):
        add_pair(o)
        xy_copy(0, o).start()

    def z_peer(k):
        return (z + k) % rep

    def part_at(s, q):
        return pl.ds(pl.multiple_of(s * chunk_lin + q * part, part), part)

    def zr_copy(s, k, wait=False):
        if parts > 1:
            src, slot = acc.at[part_at(s, z_peer(k))], k - 1
        else:
            src, slot = acc.at[part_at(s, 0)], (z + rep - k) % rep if wait else z
        return pltpu.make_async_remote_copy(
            src, z_buf.at[s, slot], zr_s.at[s, k - 1], zr_r.at[s, k - 1], device_id={"rep": z_peer(k)},
        )

    def zg_copy(s, k, wait=False):
        at = part_at(s, (z + rep - k) % rep if wait else z)
        return pltpu.make_async_remote_copy(
            full.at[at], full.at[at], zg_s.at[s, k - 1], zg_r.at[s, k - 1], device_id={"rep": z_peer(k)},
        )

    def sum_chips(s):
        def add_chip(o, total):
            xy_copy(s, o).wait_recv()
            return total + xy_buf[s, o]

        total = lax.fori_loop(0, chips - 1, add_chip, grad[chunk_rows(me, s), :])
        for h in range(per):
            acc[pl.ds(s * chunk_lin + h, chunk_lin // per, stride=per), :] = total[:, h * LANES : (h + 1) * LANES]
        for k in range(1, rep):
            zr_copy(s, k).start()

    def sum_replicas(s):
        if parts > 1:
            own = acc[part_at(s, z), :]
            for k in range(1, rep):
                zr_copy(s, k, True).wait_recv()
                own = own + z_buf[s, k - 1]
            full[part_at(s, z), :] = own
            for k in range(1, rep):
                zg_copy(s, k).start()
        else:
            z_buf[s, z] = acc[part_at(s, 0), :]
            for k in range(1, rep):
                zr_copy(s, k, True).wait_recv()
            own = z_buf[s, 0]
            for k in range(1, rep):
                own = own + z_buf[s, k]
            full[part_at(s, 0), :] = own

    def lin_at(s, owner=0):
        return pl.ds(pl.multiple_of(owner * lin + s * chunk_lin, chunk_lin), chunk_lin)

    def place(owner, s):
        return ow.at[lin_at(s, owner), :]

    def ag_copy(s, j, wait=False):
        at = place((g + chips - j) % chips * 2 + core if wait else me, s)
        return pltpu.make_async_remote_copy(
            at, at, ag_s.at[s, j], ag_r.at[s, j], device_id={"dp": (g + j) % chips * 2 + core},
        )

    def to_copy(s, j, wait=False):
        at = place((g + chips - j) % chips * 2 + (1 - core if wait else core), s)
        return pltpu.make_async_remote_copy(
            at, at, to_s.at[s, j], to_r.at[s, j], device_id={"dp": partner},
        )

    def ow_copy(s, b):
        at = lin_at(s, b)
        return pltpu.make_async_copy(ow.at[at, :], ow_hbm.at[at, :], ow_sem.at[s, b])

    def outs(s):
        at = lin_at(s)
        return [
            pltpu.make_async_copy(src.at[at, :], dst.at[at, :], out_sem.at[s, i])
            for i, (src, dst) in enumerate([(oma, oma_hbm), (om1, om1_hbm), (om2, om2_hbm)])
        ]

    def update(s):
        if parts > 1:
            for k in range(1, rep):
                zg_copy(s, k, True).wait_recv()
        at = lin_at(s)
        new_master, new_first, new_second = adam(full[at, :], ma[at, :], m1[at, :], m2[at, :])
        ow[lin_at(s, me), :] = new_master.astype(jnp.bfloat16)
        loop(1, chips, lambda j: ag_copy(s, j).start())
        to_copy(s, 0).start()
        oma[at, :] = new_master
        om1[at, :] = new_first
        om2[at, :] = new_second
        for c in outs(s):
            c.start()

    def hand_on(s):
        def one(j):
            ag_copy(s, j, True).wait_recv()
            to_copy(s, j).start()

        loop(1, chips, one)

    def store(s):
        loop(0, chips, lambda j: to_copy(s, j, True).wait_recv())
        loop(0, dp, lambda b: ow_copy(s, b).start())

    def follow(s):
        def one(o):
            if s > 1:
                xy_copy(s - 2, o).wait_send()
            xy_copy(s, o).start()

        loop(0, chips - 1, one)

    def produce(o):
        i = chip_at(o)
        if whole:
            tile(i * 2 + 1 - core)
        pair_copy(o).start()
        if whole:
            tile(i * 2 + core)

    def produce_and_send(o):
        produce(o)
        send_on(o - 1)

    produce(0)
    loop(1, chips, produce_and_send)
    add_pair(chips - 1)
    for c in loads[4:]:
        c.wait()
    if chunks > 1:
        follow(1)
    for t in range(chunks + 4):
        if t + 2 < chunks:
            follow(t + 2)
        for late, stage in enumerate((sum_chips, sum_replicas, update, hand_on, store)):
            if 0 <= t - late < chunks:
                stage(t - late)

    loop(0, chips, lambda o: pair_copy(o).wait_send())
    for s in range(max(chunks - 2, 0), chunks):
        loop(0, chips - 1, lambda o: xy_copy(s, o).wait_send())
    for s in range(chunks):
        for k in range(1, rep):
            zr_copy(s, k).wait_send()
            if parts > 1:
                zg_copy(s, k).wait_send()
        loop(1, chips, lambda j: ag_copy(s, j).wait_send())
        loop(0, chips, lambda j: to_copy(s, j).wait_send())
        loop(0, dp, lambda b: ow_copy(s, b).wait())
        for c in outs(s):
            c.wait()


def results_kernel(*refs):
    n = len(refs) // 3
    ins, outs, held, (in_sem, out_sem) = refs[:n], refs[n : 2 * n], refs[2 * n : 3 * n], refs[3 * n :]
    loads, stores = [], []
    for i in range(n):
        size = ins[i].shape[0] // PIECES
        for p in range(PIECES):
            at = pl.ds(p * size, size)
            loads.append(pltpu.make_async_copy(ins[i].at[at, :], held[i].at[at, :], in_sem.at[i, p]))
            stores.append(pltpu.make_async_copy(held[i].at[at, :], outs[i].at[at, :], out_sem.at[i, p]))
    for c in loads:
        c.start()
    for load, store in zip(loads, stores):
        load.wait()
        store.start()
    for c in stores:
        c.wait()


def shards(dp, rep, clips, cotangent, alphas, weights, master, first_moment, second_moment):
    frames, ch = clips.shape[1:]
    params = weights.shape[0]
    own = master.shape[0]
    rows = own // ch
    lin = own // LANES
    chips = dp // 2
    whole = rows == ch
    chunks = CHUNKS if whole else 1
    parts = rep if lin // chunks % (16 * rep) == 0 else 1
    part = lin // chunks // parts
    plan = (frames, ch, dp, rep, rows, whole, chunks, parts)
    anywhere = pl.BlockSpec(memory_space=pl.ANY)
    f32, bf16 = jnp.float32, jnp.bfloat16
    dma = pltpu.SemaphoreType.DMA
    outs = pl.pallas_call(
        functools.partial(step_kernel, plan),
        out_shape=(
            jax.ShapeDtypeStruct((params // LANES, LANES), bf16),
            jax.ShapeDtypeStruct((lin, LANES), f32),
            jax.ShapeDtypeStruct((lin, LANES), f32),
            jax.ShapeDtypeStruct((lin, LANES), f32),
        ),
        in_specs=[anywhere] * 7,
        out_specs=(anywhere,) * 4,
        scratch_shapes=[
            pltpu.VMEM((frames, ch), bf16),
            pltpu.VMEM((frames, ch), bf16),
            pltpu.VMEM(alphas.shape, f32),
            pltpu.VMEM((params // LANES, LANES), bf16),
            pltpu.VMEM((params // LANES, LANES), f32),
            pltpu.VMEM((params // ch, ch), bf16),
            pltpu.VMEM((lin, LANES), f32),
            pltpu.VMEM((lin, LANES), f32),
            pltpu.VMEM((lin, LANES), f32),
            pltpu.VMEM((ch // LANES, frames + 32, LANES), f32),
            pltpu.VMEM((frames, (TAPS + 1) * ch), bf16),
            pltpu.VMEM((frames, ch), f32),
            pltpu.VMEM((frames, ch), f32),
            pltpu.VMEM((frames, ch), bf16),
            pltpu.VMEM((2, ch, frames), bf16),
            pltpu.VMEM((params // ch, ch), f32),
            pltpu.VMEM((chips, rows, ch), f32),
            pltpu.VMEM((chunks, chips - 1, rows // chunks, ch), f32),
            pltpu.VMEM((lin, LANES), f32),
            pltpu.VMEM((chunks, rep, part, LANES), f32),
            pltpu.VMEM((lin, LANES), f32),
            pltpu.VMEM((params // LANES, LANES), bf16),
            pltpu.VMEM((lin, LANES), f32),
            pltpu.VMEM((lin, LANES), f32),
            pltpu.VMEM((lin, LANES), f32),
            dma((7,)),
            dma((chunks, 3)),
            dma((chunks, dp)),
            dma((chips,)), dma((chips,)),
            dma((chunks, chips)), dma((chunks, chips)),
            dma((chunks, rep)), dma((chunks, rep)),
            dma((chunks, rep)), dma((chunks, rep)),
            dma((chunks, chips)), dma((chunks, chips)),
            dma((chunks, chips)), dma((chunks, chips)),
        ],
        compiler_params=pltpu.CompilerParams(
            collective_id=0, has_side_effects=True, vmem_limit_bytes=64 * 1024 * 1024
        ),
        name="train_step",
    )(
        clips[0],
        cotangent[0],
        alphas,
        weights.reshape(params // LANES, LANES),
        master.reshape(lin, LANES),
        first_moment.reshape(lin, LANES),
        second_moment.reshape(lin, LANES),
    )
    outs = pl.pallas_call(
        results_kernel,
        out_shape=tuple(jax.ShapeDtypeStruct(o.shape, o.dtype) for o in outs),
        in_specs=[anywhere] * len(outs),
        out_specs=(anywhere,) * len(outs),
        scratch_shapes=[pltpu.VMEM(o.shape, o.dtype) for o in outs] + [dma((len(outs), PIECES))] * 2,
        compiler_params=pltpu.CompilerParams(vmem_limit_bytes=64 * 1024 * 1024),
        name="results",
    )(*outs)
    return tuple(o.reshape(-1) for o in outs)


def solution(mesh):
    return jax.shard_map(
        functools.partial(shards, mesh.shape["dp"], mesh.shape["rep"]),
        mesh=mesh,
        in_specs=(
            P(("dp", "rep"), None, None),
            P(("dp", "rep"), None, None),
            P(),
            P(),
            P("dp"),
            P("dp"),
            P("dp"),
        ),
        out_specs=(P(), P("dp"), P("dp"), P("dp")),
        check_vma=False,
    )
```
